32 devices in a mesh: seq: 4 (over z), ctx: 8 (over y, x, core).
Axes of the slice: x: 2, y: 2, z: 4, core: 2. Of those that a mesh axis runs over, the one named last changes fastest.
Arguments:
- layer_in: bfloat16 [4, 1024, 2048], P('seq', 'ctx'), may hold values from -6 to 6
- cotangent: bfloat16 [4, 1024, 2048], P('seq', 'ctx'), may hold values from -6 to 6
- file_lengths: int32 [4, 8], P('seq'), may hold values from 1 to 1017, as said below
- routes: int32 [4, 1024, 8], P('seq', 'ctx'), may hold values from 0 to 63, all different within a row; in each aligned block of 128 rows (0 to 127, 128 to 255, ..., all dimensions but the last counted through in order) at most 32 rows name the same one
- attn_gain: bfloat16 [2048], P(('seq', 'ctx')), may hold values from 0.25 to 1.75
- q_gain: bfloat16 [2048], P(('seq', 'ctx')), may hold values from 0.25 to 1.75
- k_gain: bfloat16 [2048], P(('seq', 'ctx')), may hold values from 0.25 to 1.75
- ffn_gain: bfloat16 [2048], P(('seq', 'ctx')), may hold values from 0.25 to 1.75
- w_q: bfloat16 [2048, 2048], P(('seq', 'ctx')), may hold values from -0.125 to 0.125
- w_k: bfloat16 [2048, 2048], P(('seq', 'ctx')), may hold values from -0.125 to 0.125
- w_v: bfloat16 [2048, 2048], P(('seq', 'ctx')), may hold values from -0.125 to 0.125
- w_o: bfloat16 [2048, 2048], P(('seq', 'ctx')), may hold values from -2 to 2
- router: bfloat16 [2048, 64], P(('seq', 'ctx')), may hold values from -0.0625 to 0.0625
- expert_gate: bfloat16 [64, 2048, 1024], P('seq', 'ctx'), may hold values from -0.125 to 0.125
- expert_up: bfloat16 [64, 2048, 1024], P('seq', 'ctx'), may hold values from -0.125 to 0.125
- expert_down: bfloat16 [64, 1024, 2048], P('seq', 'ctx'), may hold values from -6 to 6
Outputs:
- layer_out: bfloat16 [4, 1024, 2048], P('seq', 'ctx')
- input_grad: bfloat16 [4, 1024, 2048], P('seq', 'ctx')
- attn_gain_grad: float32 [2048], P(('seq', 'ctx'))
- q_gain_grad: float32 [2048], P(('seq', 'ctx'))
- k_gain_grad: float32 [2048], P(('seq', 'ctx'))
- ffn_gain_grad: float32 [2048], P(('seq', 'ctx'))
- w_q_grad: float32 [2048, 2048], P(('seq', 'ctx'))
- w_k_grad: float32 [2048, 2048], P(('seq', 'ctx'))
- w_v_grad: float32 [2048, 2048], P(('seq', 'ctx'))
- w_o_grad: float32 [2048, 2048], P(('seq', 'ctx'))
- router_grad: float32 [2048, 64], P(('seq', 'ctx'))
- expert_gate_grad: float32 [64, 2048, 1024], P('seq', 'ctx')
- expert_up_grad: float32 [64, 2048, 1024], P('seq', 'ctx')
- expert_down_grad: float32 [64, 1024, 2048], P('seq', 'ctx')
- expert_counts: int32 [32, 64], replicated
The draws below stay inside these ranges and needn't reach their ends.
Inputs may be any that keep to these rules, and one draw needn't show every extreme that they name: `file_lengths`: each row holds the lengths of the 8 files of one sequence in order and sums to 1024; in every row one file starts within the first 128 positions and ends within the last 128; in some row all other files have length 1. `routes`: each row names 8 different experts. In each aligned block of 128 rows (the tokens of one device) no expert is named by more than 32 rows, and in some block an expert is named by exactly 32 rows; every expert is named somewhere.
All inputs are finite; a program needn't handle non-finite values.
Results may differ from the reference program's by a relative error of at most 0.029.
Values may be sent and summed in bfloat16 or wider, within the bound.
No kernel may reach another device: no remote copies, remote signals or barrier semaphores. Data moves between devices by JAX's collectives and lax.ppermute only.
A program may use at most 448 MiB of HBM per device.

```python
import math
import jax
import jax.numpy as jnp
import numpy as np
from jax import lax

D = 2048
HEADS = 16
HEAD_DIM = 128
EXPERTS = 64
FF = 1024
TOPK = 8
TOK_DEV = 128
FILES = 8
SEQS = 4
LENGTH = 1024
CAP = 32


def draw_file_lengths(key, part):
    key = jax.random.fold_in(key, 11)
    first_key, second_key, third_key = jax.random.split(key, 3)
    short = (TOK_DEV - 1) // (FILES - 1)
    others = jax.random.randint(first_key, (SEQS, FILES), 1, short + 1, dtype=jnp.int32)
    where_long = jax.random.randint(second_key, (SEQS, 1), 0, FILES, dtype=jnp.int32)
    tight_row = jax.random.randint(third_key, (), 0, SEQS, dtype=jnp.int32)
    row_index = jnp.arange(SEQS, dtype=jnp.int32)[:, None]
    others = jnp.where(row_index == tight_row, 1, others)
    column = jnp.arange(FILES, dtype=jnp.int32)[None, :]
    rest = jnp.sum(jnp.where(column == where_long, 0, others), axis=1, keepdims=True)
    return jnp.where(column == where_long, LENGTH - rest, others).astype(jnp.int32)


def raised(drawn, stream_key, source, target, parts, factor):
    owner, partner = [(jnp.arange(drawn.shape[dim]) // (drawn.shape[dim] // parts)).reshape([-1 if axis == dim else 1 for axis in range(drawn.ndim)]) for dim in (source, target)]
    chosen = jax.random.permutation(stream_key, parts)[partner]
    strong = (owner == chosen) | (owner == (partner + parts // 2) % parts)
    return jnp.where(strong, factor * drawn, drawn)


def levels(key, extent, shards, least, top_value):
    factor_of, own = 1.0, jax.random.fold_in(key, 6)
    for dim, blocks in shards:
        steps = jnp.exp(jax.random.uniform(jax.random.fold_in(own, dim), (blocks,), jnp.float32, least / len(shards), top_value / len(shards)))
        factor_of = factor_of * jnp.repeat(steps, extent[dim] // blocks).reshape([-1 if axis == dim else 1 for axis in range(len(extent))])
    return factor_of


def routed_block(key, own, number, rows, amount, top, bound, lean):
    sequence = jax.random.permutation(key, amount)
    packed, ordinary = portions_of(amount, rows * top, bound, lean, True), portions_of(amount, rows * top, bound, lean, False)
    places = jnp.arange(amount)

    def named(sizes, rotation):
        used = int((sizes > 0).sum())
        fixed = max(1, used // 4)
        moved = fixed + (places - fixed + rotation * (used - fixed)) % max(1, amount - fixed)
        return jnp.zeros((amount,), jnp.int32).at[sequence[jnp.where(places < fixed, places, moved)]].set(jnp.asarray(sizes, jnp.int32))

    sizes = jnp.where(number % 4 == 0, named(packed, number // 4), named(ordinary, number - number // 4 - 1))
    mixed = jax.random.permutation(jax.random.fold_in(own, 3), amount)
    source_of, sink = mixed[0:amount // 2 * 2:2], mixed[1:amount // 2 * 2:2]
    room = jnp.minimum(sizes[source_of] - 1, bound - sizes[sink]) // 2
    room = jnp.where((source_of == sequence[0]) | (sink == sequence[0]) | (sizes[sink] == 0), 0, jnp.maximum(room, 0))
    moved = jax.random.randint(jax.random.fold_in(own, 4), (amount // 2,), 0, 1 << 20) % (room + 1)
    sizes = sizes.at[source_of].add(-moved).at[sink].add(moved)
    labels = jnp.searchsorted(jnp.cumsum(sizes), jnp.arange(rows * top), side="right").astype(jnp.int32)
    grid = labels.reshape(top, rows).T
    grid = grid[jax.random.permutation(jax.random.fold_in(own, 1), rows)]
    rotation = jax.random.randint(jax.random.fold_in(own, 2), (rows, 1), 0, top)
    return jnp.take_along_axis(grid, (jnp.arange(top)[None, :] + rotation) % top, axis=1)


def portions_of(amount, total, bound, lean, full):
    portions = [(1 << 20) // math.isqrt(standing ** lean) + 1 for standing in range(1, amount + 1)]
    largest = bound if full else min(bound, max(-(-total // amount), total * portions[0] // sum(portions)))
    least = 1 if total - largest >= amount - 1 else 0
    given, spare = [largest] + [least] * (amount - 1), total - largest - least * (amount - 1)
    while spare > 0:
        movable = [i for i in range(1, amount) if given[i] < largest] or [i for i in range(1, amount) if given[i] < bound]
        mass, remaining = sum([portions[i] for i in movable]), spare
        for i in movable:
            addition = min(bound - given[i], max(1, remaining * portions[i] // mass), spare)
            given[i] = given[i] + addition
            spare = spare - addition
    return np.array(given)


def bell_draw(key, extent, deviation, most, pieces=(), kind=jnp.bfloat16):
    gain = levels(key, extent, pieces, -0.22, 0.18) if pieces else 1.0
    drawn = jax.random.normal(key, extent, jnp.float32) * deviation * gain
    return jnp.minimum(jnp.maximum(drawn, -most), most).astype(kind)


def gaussian_with(stream_key, dims, spread, reach, cuts, heavy, kind=jnp.bfloat16):
    array = spread * jax.random.normal(stream_key, dims, jnp.float32)
    if cuts:
        array = array * levels(stream_key, dims, cuts, -0.22, 0.18)
    return jnp.clip(raised(array, jax.random.fold_in(stream_key, 3), *heavy), -reach, reach).astype(kind)


def setup_inputs(seed: int = 0) -> dict:
    streams_of = jax.random.split(jax.random.key(seed), 17)
    layer_in = gaussian_with(streams_of[0], (SEQS, LENGTH, D), 1.0, 6.0, ((0, 4), (1, 8)), (1, 2, 8, 2.0))
    cotangent = bell_draw(streams_of[1], (SEQS, LENGTH, D), 1.0, 6.0, ((0, 4), (1, 8)))
    file_lengths = draw_file_lengths(jax.random.fold_in(streams_of[16], 71), 0)
    routes_keys = jax.random.split(jax.random.fold_in(streams_of[3], 1), SEQS * LENGTH // TOK_DEV)
    routes_turns = jax.random.permutation(jax.random.fold_in(streams_of[3], 3), SEQS * LENGTH // TOK_DEV)
    routes = jax.vmap(lambda own, number: routed_block(jax.random.fold_in(streams_of[3], 2), own, number, TOK_DEV, EXPERTS, TOPK, CAP, 1))(routes_keys, routes_turns).reshape((SEQS, LENGTH, TOPK))
    attn_gain = jnp.clip(1.0 + 0.15 * jax.random.normal(streams_of[4], (D,), jnp.float32), 0.25, 1.75).astype(jnp.bfloat16)
    q_gain = jnp.clip(1.0 + 0.15 * jax.random.normal(streams_of[5], (D,), jnp.float32), 0.25, 1.75).astype(jnp.bfloat16)
    k_gain = jnp.clip(1.0 + 0.15 * jax.random.normal(streams_of[6], (D,), jnp.float32), 0.25, 1.75).astype(jnp.bfloat16)
    ffn_gain = jnp.clip(1.0 + 0.15 * jax.random.normal(streams_of[7], (D,), jnp.float32), 0.25, 1.75).astype(jnp.bfloat16)
    w_q = bell_draw(streams_of[8], (D, D), D ** -0.5, 0.125, ((0, 32),))
    w_k = bell_draw(streams_of[9], (D, D), D ** -0.5, 0.125, ((0, 32),))
    w_v = bell_draw(streams_of[10], (D, D), D ** -0.5, 0.125, ((0, 32),))
    w_o = bell_draw(streams_of[11], (D, D), (max(D // 256, 1)) ** -0.5, 2.0, ((0, 32),))
    router = bell_draw(streams_of[12], (D, EXPERTS), (4 * D) ** -0.5, 0.0625, ((0, 32),))
    expert_gate = bell_draw(streams_of[13], (EXPERTS, D, FF), D ** -0.5, 0.125, ((0, 4), (1, 8)))
    expert_up = bell_draw(streams_of[14], (EXPERTS, D, FF), D ** -0.5, 0.125, ((0, 4), (1, 8)))
    expert_down = bell_draw(streams_of[15], (EXPERTS, FF, D), (max(FF // 1024, 1)) ** -0.5, 6.0, ((0, 4), (1, 8)))
    return {"layer_in": layer_in, "cotangent": cotangent, "file_lengths": file_lengths, "routes": routes, "attn_gain": attn_gain, "q_gain": q_gain, "k_gain": k_gain, "ffn_gain": ffn_gain, "w_q": w_q, "w_k": w_k, "w_v": w_v, "w_o": w_o, "router": router, "expert_gate": expert_gate, "expert_up": expert_up, "expert_down": expert_down}


@jax.custom_vjp
def low(v):
    return lax.optimization_barrier(v.astype(jnp.bfloat16)).astype(jnp.float32)

@jax.custom_vjp
def low_back(v):
    return v

def low_keep(v):
    return (low(v), None)

def low_pass(kept, grad):
    return (grad,)

def back_keep(v):
    return (v, None)

def back_low(kept, grad):
    return (low(grad),)
low.defvjp(low_keep, low_pass)
low_back.defvjp(back_keep, back_low)
EPS = 1e-05
NEG = -1e+30
HIGH = lax.Precision.HIGHEST

def rms_scale(values):
    return lax.rsqrt(lax.optimization_barrier(jnp.mean(values * values, axis=-1, keepdims=True)) + EPS)

def angles(positions):
    half = HEAD_DIM // 2
    inverse = 10000.0 ** (-(jnp.arange(half, dtype=jnp.float32) * 2.0 / HEAD_DIM))
    theta = positions.astype(jnp.float32)[:, None] * inverse[None, :]
    return (jnp.cos(theta)[:, None, :], jnp.sin(theta)[:, None, :])

def rotate(values, cosine, sine):
    half = values.shape[-1] // 2
    first = values[..., :half]
    second = values[..., half:]
    return jnp.concatenate([first * cosine - second * sine, second * cosine + first * sine], axis=-1)

def segments(offsets, positions):
    return lax.optimization_barrier(jnp.sum((positions[:, None] >= offsets[None, :]).astype(jnp.int32), axis=1)) - 1

def attend_sequence(seq_input, lengths, params):
    gain_attn, gain_query, gain_key, query_weight, key_weight, value_weight, out_weight = params
    length = seq_input.shape[0]
    hidden = low(seq_input * rms_scale(seq_input) * gain_attn)
    query_lin = low_back(jnp.dot(hidden, query_weight, precision=HIGH))
    key_lin = low_back(jnp.dot(hidden, key_weight, precision=HIGH))
    value_lin = low_back(jnp.dot(hidden, value_weight, precision=HIGH))
    positions = jnp.arange(length, dtype=jnp.int32)
    cosine, sine = angles(positions)
    queries = low(rotate((query_lin * rms_scale(query_lin) * gain_query).reshape(length, HEADS, HEAD_DIM), cosine, sine))
    keys = low(rotate((key_lin * rms_scale(key_lin) * gain_key).reshape(length, HEADS, HEAD_DIM), cosine, sine))
    values = low(value_lin.reshape(length, HEADS, HEAD_DIM))
    offsets = jnp.cumsum(lengths) - lengths
    files = segments(offsets, positions)
    block = min(512, length)

    def query_block(number):
        first = (number * block).astype(jnp.int32)
        block_queries = lax.dynamic_slice_in_dim(queries, first, block, 0)
        block_pos = first + jnp.arange(block, dtype=jnp.int32)
        block_files = lax.dynamic_slice_in_dim(files, first, block, 0)
        allowed = (positions[None, :] <= block_pos[:, None]) & (files[None, :] == block_files[:, None])
        scores = low_back(jnp.einsum('qhd,khd->hqk', block_queries, keys, precision=HIGH) * HEAD_DIM ** (-0.5))
        scores = jnp.where(allowed[None], scores, NEG)
        top = lax.optimization_barrier(jnp.max(scores, axis=-1, keepdims=True))
        shifted = jnp.exp(scores - top)
        weights = low(shifted / lax.optimization_barrier(jnp.sum(shifted, axis=-1, keepdims=True)))
        return jnp.einsum('hqk,khd->qhd', weights, values, precision=HIGH)
    attended = lax.map(jax.checkpoint(query_block), jnp.arange(length // block, dtype=jnp.int32))
    mixed = low(low_back(attended.reshape(length, HEADS * HEAD_DIM)))
    return seq_input + low_back(jnp.dot(mixed, out_weight, precision=HIGH))

def route_slots(picks):
    flat = picks.reshape(-1)
    one_hot = (flat[:, None] == jnp.arange(EXPERTS, dtype=jnp.int32)[None, :]).astype(jnp.int32)
    rank = lax.optimization_barrier(jnp.sum(one_hot * jnp.cumsum(one_hot, axis=0), axis=1)) - 1
    owner = jnp.arange(flat.shape[0], dtype=jnp.int32) // TOPK
    return (flat * CAP + rank, owner)

def expert_block(resid, picks, params):
    gain_ffn, router_weight, gate_weight, up_weight, down_weight = params
    tokens = resid.shape[0]
    normed = low(resid * rms_scale(resid) * gain_ffn)
    logits = low_back(jnp.dot(normed, router_weight, precision=HIGH))
    shifted = jnp.exp(logits - lax.optimization_barrier(jnp.max(logits, axis=-1, keepdims=True)))
    router_probs = shifted / lax.optimization_barrier(jnp.sum(shifted, axis=-1, keepdims=True))
    chosen = jnp.take_along_axis(router_probs, picks, axis=1)
    slot, owner = route_slots(picks)
    rows = jnp.zeros((EXPERTS * CAP, D), jnp.float32).at[slot].set(normed[owner])
    rows = low_back(rows).reshape(EXPERTS, CAP, D)
    gate_val = low_back(jnp.einsum('ecd,edf->ecf', rows, gate_weight, precision=HIGH))
    up_val = low_back(jnp.einsum('ecd,edf->ecf', rows, up_weight, precision=HIGH))
    active = low(gate_val * jax.nn.sigmoid(gate_val) * up_val)
    result = low(low_back(jnp.einsum('ecf,efd->ecd', active, down_weight, precision=HIGH)))
    picked = result.reshape(EXPERTS * CAP, D)[slot].reshape(tokens, TOPK, D)
    return resid + lax.optimization_barrier(jnp.sum(chosen[:, :, None] * picked, axis=1))

def forward(inputs, params, file_lengths, routes):
    gain_attn, gain_query, gain_key, gain_ffn, query_weight, key_weight, value_weight, out_weight, router_weight, gate_weight, up_weight, down_weight = params

    def one_sequence(pair):
        return attend_sequence(pair[0], pair[1], (gain_attn, gain_query, gain_key, query_weight, key_weight, value_weight, out_weight))
    resid = lax.map(jax.checkpoint(one_sequence), (inputs, file_lengths))
    blocks = resid.reshape(-1, TOK_DEV, D)
    pick_blocks = routes.reshape(-1, TOK_DEV, TOPK)

    def one_block(pair):
        return expert_block(pair[0], pair[1], (gain_ffn, router_weight, gate_weight, up_weight, down_weight))
    output = lax.map(jax.checkpoint(one_block), (blocks, pick_blocks))
    return output.reshape(inputs.shape)

def reference(layer_in, cotangent, file_lengths, routes, attn_gain, q_gain, k_gain, ffn_gain, w_q, w_k, w_v, w_o, router, expert_gate, expert_up, expert_down):
    params = (attn_gain.astype(jnp.float32), q_gain.astype(jnp.float32), k_gain.astype(jnp.float32), ffn_gain.astype(jnp.float32), w_q.astype(jnp.float32), w_k.astype(jnp.float32), w_v.astype(jnp.float32), w_o.astype(jnp.float32), router.astype(jnp.float32), expert_gate.astype(jnp.float32), expert_up.astype(jnp.float32), expert_down.astype(jnp.float32))

    def wrapped(inputs, weights):
        return forward(inputs, weights, file_lengths, routes)
    output, pullback = jax.vjp(wrapped, layer_in.astype(jnp.float32), params)
    grad_input, grads = pullback(cotangent.astype(jnp.float32))
    block_routes = routes.reshape(-1, TOK_DEV * TOPK)
    counts = lax.optimization_barrier(jnp.sum((block_routes[:, :, None] == jnp.arange(EXPERTS, dtype=jnp.int32)[None, None, :]).astype(jnp.int32), axis=1))
    return (output.astype(jnp.bfloat16), grad_input.astype(jnp.bfloat16), grads[0], grads[1], grads[2], grads[3], grads[4], grads[5], grads[6], grads[7], grads[8], grads[9], grads[10], grads[11], counts)
```

```python
import jax
import jax.numpy as jnp
import numpy as np
from jax import lax
from jax.experimental import pallas as pl
from jax.experimental.pallas import tpu as pltpu
from jax.sharding import PartitionSpec as P

HEAD_DIM = 128
CAP = 32
EPS = 1e-05
NEG = -1e30
BF = jnp.bfloat16
F32 = jnp.float32
BOTH = ("seq", "ctx")


def mm(spec, a, b):
    return jnp.einsum(spec, a, b, preferred_element_type=F32)


def angles(positions):
    half = HEAD_DIM // 2
    inverse = 10000.0 ** (-(jnp.arange(half, dtype=F32) * 2.0 / HEAD_DIM))
    theta = positions.astype(F32)[:, None] * inverse[None, :]
    return (jnp.cos(theta)[:, None, :], jnp.sin(theta)[:, None, :])


def rotate(values, cosine, sine):
    half = values.shape[-1] // 2
    first = values[..., :half]
    second = values[..., half:]
    return jnp.concatenate(
        [first * cosine - second * sine, second * cosine + first * sine], axis=-1
    )


def segments(offsets, positions):
    return jnp.sum((positions[:, None] >= offsets[None, :]).astype(jnp.int32), axis=1) - 1


def swap(value, mask):
    size = lax.axis_size("ctx")
    return lax.ppermute(value, "ctx", [(i, i ^ mask) for i in range(size)])


def shift(value):
    size = lax.axis_size("seq")
    return lax.ppermute(value, "seq", [(i, (i + 1) % size) for i in range(size)])


def to_earlier(value, offset):
    size = lax.axis_size("seq")
    if offset % size == 0:
        return value
    return lax.ppermute(value, "seq", [(i, (i - offset) % size) for i in range(size)])


def subsets(bits):
    out = []
    for number in range(1 << len(bits)):
        mask = 0
        for place, bit in enumerate(reversed(bits)):
            mask |= (number >> place & 1) << bit
        out.append(mask)
    return out


def coordinate(index, bits):
    out = jnp.int32(0)
    for bit in bits:
        out = out * 2 + (lax.shift_right_logical(index, bit) & 1)
    return out


def mark(*arrays):
    return sum(array[(0,) * array.ndim].astype(F32) * 0.0 for array in arrays)


def pick(value, index, axis):
    return lax.dynamic_index_in_dim(value, index, axis, keepdims=False)


def held(value, zero):
    return value + zero.astype(value.dtype)


class Plan:
    def __init__(self, number, split, shared, size, me):
        self.split = subsets(split)
        self.masks = subsets(shared)
        self.count = len(self.masks)
        self.each = size // self.count
        self.place = coordinate(me, shared)
        self.first = number * size
        self.experts = jnp.concatenate(
            [
                self.first + (self.place ^ o) * self.each + jnp.arange(self.each, dtype=jnp.int32)
                for o in range(self.count)
            ]
        )
        self.others = jnp.concatenate(
            [jnp.full((self.each,), me ^ self.masks[o], jnp.int32) for o in range(self.count)]
        )


def exchange_blocks(value, other, block):
    parts = [value[:, i * block : (i + 1) * block] for i in range(value.shape[1] // block)]
    turned = jnp.concatenate([parts[i ^ 1] for i in range(len(parts))], axis=1)
    return jnp.where(other & 1 == 1, turned, value)


def take_blocks(part, order):
    count = order.shape[0]
    blocks = part.reshape(part.shape[:-1] + (count, part.shape[-1] // count))
    return jnp.take(blocks, order, axis=-2).reshape(part.shape)


def pack(arrays, plans, block, ranks):
    total = len(arrays)
    rows, cols = arrays[0].shape[1:]
    each, count = plans[0].each, plans[0].count
    pieces = len(plans) * count
    experts = jnp.concatenate([plan.experts for plan in plans])
    others = jnp.concatenate([plan.others for plan in plans])
    if block % 128:
        out = []
        for number in range(pieces):
            few = experts[number * each : (number + 1) * each]
            part = jnp.stack([array[few] for array in arrays], axis=1)
            order = jnp.arange(ranks, dtype=jnp.int32) ^ (others[number * each] & 1)
            out.append(take_blocks(part, order))
        return out

    def kernel(experts_ref, others_ref, *refs):
        step = pl.program_id(0)
        for i in range(total):
            value = refs[i][0]
            if block:
                value = exchange_blocks(value, others_ref[step], block)
            for number in range(pieces):

                @pl.when(step // each == number)
                def _():
                    refs[total + number][0, i] = value

    def out_spec(number):
        return pl.BlockSpec(
            (1, total, rows, cols),
            lambda step, e, t: (jnp.clip(step - number * each, 0, each - 1), 0, 0, 0),
        )

    return pl.pallas_call(
        kernel,
        grid_spec=pltpu.PrefetchScalarGridSpec(
            num_scalar_prefetch=2,
            grid=(pieces * each,),
            in_specs=[pl.BlockSpec((1, rows, cols), lambda step, e, t: (e[step], 0, 0))] * total,
            out_specs=[out_spec(number) for number in range(pieces)],
        ),
        out_shape=[jax.ShapeDtypeStruct((each, total, rows, cols), BF)] * pieces,
        compiler_params=pltpu.CompilerParams(vmem_limit_bytes=48 << 20),
        cost_estimate=pl.CostEstimate(
            flops=0, bytes_accessed=4 * total * arrays[0].size, transcendentals=0
        ),
        name="pack",
    )(experts, others, *arrays)


def unpack(parts, plans, block, ranks, wait):
    each, total, rows, cols = parts[0].shape
    count = plans[0].count
    pieces = len(parts)
    experts = jnp.concatenate([plan.experts for plan in plans])
    others = jnp.concatenate([plan.others for plan in plans])
    if block % 128:
        out = [jnp.zeros((pieces * each, rows, cols), F32)] * total
        for number in range(pieces):
            order = jnp.arange(ranks, dtype=jnp.int32) ^ (others[number * each] & 1)
            part = take_blocks(parts[number], order).astype(F32)
            out = [
                lax.dynamic_update_slice_in_dim(out[i], part[:, i], experts[number * each], 0)
                for i in range(total)
            ]
        return out

    def kernel(experts_ref, others_ref, *refs):
        step = pl.program_id(0)
        for number in range(pieces):

            @pl.when(step // each == number)
            def _():
                for i in range(total):
                    value = refs[number][0, i]
                    if block:
                        value = exchange_blocks(value, others_ref[step], block)
                    refs[pieces + len(wait) + i][0] = value.astype(F32)

    def in_spec(number):
        return pl.BlockSpec(
            (1, total, rows, cols),
            lambda step, e, t: (jnp.clip(step - number * each, 0, each - 1), 0, 0, 0),
        )

    return pl.pallas_call(
        kernel,
        grid_spec=pltpu.PrefetchScalarGridSpec(
            num_scalar_prefetch=2,
            grid=(pieces * each,),
            in_specs=[in_spec(number) for number in range(pieces)]
            + [pl.BlockSpec(memory_space=pl.ANY)] * len(wait),
            out_specs=[pl.BlockSpec((1, rows, cols), lambda step, e, t: (e[step], 0, 0))] * total,
        ),
        out_shape=[jax.ShapeDtypeStruct((pieces * each, rows, cols), F32)] * total,
        compiler_params=pltpu.CompilerParams(vmem_limit_bytes=48 << 20),
        cost_estimate=pl.CostEstimate(
            flops=0, bytes_accessed=6 * total * pieces * each * rows * cols, transcendentals=0
        ),
        name="unpack",
    )(experts, others, *parts, *wait)


def send_piece(part, number, plans):
    count = plans[0].count
    mask = plans[number // count].masks[number % count]
    return swap(part, mask) if mask else part


def send_pieces(parts, plans):
    return [send_piece(part, number, plans) for number, part in enumerate(parts)]


def window(ref, start, size):
    last = ref.shape[0] - 64
    return jnp.concatenate(
        [
            ref[pl.ds(pl.multiple_of(jnp.minimum(start + i, last), 16), 64), :]
            for i in range(0, size, 64)
        ],
        axis=0,
    )


def store_rows(ref, start, used, value, first=0):
    for i in range(0, value.shape[0], 64):

        @pl.when(used > i)
        def _():
            rows = pl.ds(pl.multiple_of(start + i, 16), 64)
            ref[rows, first : first + value.shape[1]] = value[i : i + 64].astype(ref.dtype)


class Experts:
    def __init__(self, plan, ranks, tokens, wide, ff, width, planes, room, layout):
        self.plan, self.ranks, self.tokens, self.wide = plan, ranks, tokens, wide
        self.ff, self.width, self.planes, self.room = ff, width, planes, room
        self.each, self.count = plan.each, plan.count
        self.ff_own = ff // len(plan.split)
        self.ff_wide = ff // ranks
        self.size = ranks * CAP
        self.length = ranks * tokens
        self.scalars, self.slot_at, self.select, self.select_t = layout

    def call(self, kernel, name, place, me, wait, grid, ins, outs, scratch=(), flops=0):
        arrays = [entry[0] for entry in ins]
        size = sum(array.size * array.dtype.itemsize for array in arrays)
        size += sum(int(np.prod(shape)) * jnp.dtype(kind).itemsize for shape, kind, _, _ in outs)
        first, last = len(ins) + 1, len(ins) + 1 + len(wait)

        def body(*refs):
            kernel(*refs[:first], *refs[last:])

        def in_spec(block, index, once=False):
            if once:
                return pl.BlockSpec(block, index, pipeline_mode=pl.Buffered(1))
            return pl.BlockSpec(block, index)

        return pl.pallas_call(
            body,
            grid_spec=pltpu.PrefetchScalarGridSpec(
                num_scalar_prefetch=1,
                grid=(grid,),
                in_specs=[in_spec(*entry[1:]) for entry in ins]
                + [pl.BlockSpec(memory_space=pl.ANY)] * len(wait),
                out_specs=[pl.BlockSpec(block, index) for _, _, block, index in outs],
                scratch_shapes=list(scratch),
            ),
            out_shape=[jax.ShapeDtypeStruct(shape, kind) for shape, kind, _, _ in outs],
            compiler_params=pltpu.CompilerParams(vmem_limit_bytes=58 << 20),
            cost_estimate=pl.CostEstimate(flops=flops, bytes_accessed=size, transcendentals=0),
            name=name,
        )(jnp.concatenate([jnp.stack([place, me]), self.scalars]), *arrays, *wait)

    def extent(self, s_ref, place, expert):
        base = 2 + place * 2 * self.each + expert
        return s_ref[base], s_ref[base + self.each]

    def slots_in(self):
        block = (1,) + self.slot_at.shape[1:]
        return (self.slot_at, block, lambda e, s: (s[0], 0, 0, 0), True)

    def select_in(self):
        block = (self.ranks,) + self.select.shape[1:]
        return (self.select, block, lambda e, s: (s[0], 0, 0), True)

    def select_t_in(self):
        block = (self.ranks,) + self.select_t.shape[1:]
        return (self.select_t, block, lambda e, s: (s[0], 0, 0), True)

    def by_expert(self, array):
        block = (1,) + array.shape[1:]
        return (array, block, lambda e, s: (e,) + (0,) * (len(block) - 1))

    def whole(self, array, once=True):
        return (array, array.shape, lambda e, s: (0,) * array.ndim, once)

    def out_by_expert(self, shape, kind):
        block = (1,) + shape[1:]
        return (shape, kind, block, lambda e, s: (e,) + (0,) * (len(block) - 1))

    def out_whole(self, shape, kind):
        return (shape, kind, shape, lambda e, s: (0,) * len(shape))

    def packed(self, columns, kind=BF):
        return self.out_whole((self.room, columns), kind)

    def packing(self, at):
        rows = lax.broadcasted_iota(jnp.int32, (self.size, self.size), 0)
        return jnp.where(rows == at, 1.0, 0.0).astype(BF)

    def unpacked(self, at, value):
        return lax.dot_general(
            self.packing(at), value, (((0,), (0,)), ((), ())), preferred_element_type=F32
        )

    def weight_of(self, refs, i):
        return jnp.concatenate([ref[0, i] for ref in refs], axis=0)

    def cot_rows(self, wait, place, me, probs, near, far, masks, downs):
        each, count, width, tokens = self.each, self.count, self.width, self.tokens
        half, own, size = len(masks), self.ff_own, self.size
        cols = min(512, width)

        def kernel(s_ref, at_ref, sel_ref, probs_ref, near_ref, far_ref, *refs):
            down = refs[:count]
            rows_ref, base_ref, packed_ref, held_ref, sum_ref = refs[count:]
            step = pl.program_id(0)

            for number, mask in enumerate(masks):
                for side, ref in enumerate((near_ref, far_ref)):
                    held_ref[s_ref[1] ^ mask ^ side] = ref[number]
            for b in range(self.ranks):
                rows = jnp.dot(sel_ref[b], held_ref[b], preferred_element_type=F32).astype(BF)
                for e in range(each):
                    rows_ref[e, b * CAP : (b + 1) * CAP, :] = rows[e * CAP : (e + 1) * CAP]
            for e in range(each):
                weight = jnp.concatenate([ref[e, 0] for ref in down], axis=0)
                base = lax.dot_general(
                    rows_ref[e], weight, (((1,), (1,)), ((), ())), preferred_element_type=F32
                )

                @pl.when(step == 0)
                def _():
                    sum_ref[e] = base

                @pl.when(step > 0)
                def _():
                    sum_ref[e] += base

            @pl.when(step == width // cols - 1)
            def _():
                base_ref[...] = jnp.zeros_like(base_ref)
                packed_ref[...] = jnp.zeros_like(packed_ref)
                for e in range(each):
                    start, used = self.extent(s_ref, s_ref[0], e)
                    packing = self.packing(at_ref[0, e])
                    base = jnp.dot(packing, sum_ref[e].astype(BF), preferred_element_type=F32)
                    store_rows(base_ref, start, used, base.astype(BF))
                    chosen = [
                        jnp.sum(
                            sel_ref[b, e * CAP : (e + 1) * CAP, :].astype(F32)
                            * probs_ref[e : e + 1, b * tokens : (b + 1) * tokens],
                            axis=1,
                            keepdims=True,
                        )
                        for b in range(self.ranks)
                    ]
                    chosen = jnp.concatenate(chosen, axis=0).astype(BF)
                    chosen = jnp.dot(packing, chosen, preferred_element_type=F32)
                    store_rows(packed_ref, start, used, chosen)

        by_column = lambda c, s: (0, 0, c)
        ins = [self.slots_in(), self.select_in(), self.whole(probs)]
        ins += [(array, (half, tokens, cols), by_column) for array in (near, far)]
        ins += [(piece, piece.shape[:3] + (cols,), lambda c, s: (0, 0, 0, c)) for piece in downs]
        outs = [
            ((each, size, width), BF, (each, size, cols), by_column),
            self.packed(own),
            self.packed(1, F32),
        ]
        flops = 2 * each * size * width * (tokens + own)
        scratch = [
            pltpu.VMEM((self.ranks, tokens, cols), BF),
            pltpu.VMEM((each, size, own), F32),
        ]
        return self.call(
            kernel, "cot_rows", place, me, wait, width // cols, ins, outs, scratch, flops
        )

    def gate_up(self, wait, place, parts, weights, passed=()):
        each, count, wide, own, size = self.each, self.count, self.wide, self.ff_own, self.size
        tokens, chips = self.tokens, len(self.plan.split)

        def kernel(s_ref, at_ref, sel_ref, *refs):
            token, weight = refs[:count], refs[count : 2 * count]
            extra = refs[2 * count : 2 * count + len(passed)]
            rows_ref, value_ref, *pass_refs, held_ref = refs[2 * count + len(passed) :]
            expert = pl.program_id(0)
            start, used = self.extent(s_ref, s_ref[0], expert)

            @pl.when(expert == 0)
            def _():
                for ref, out in zip((token[0], *extra), pass_refs):
                    out[...] = ref[...]
                value_ref[...] = jnp.zeros_like(value_ref)
                for b in range(self.ranks):
                    rows_of = slice(b * tokens, (b + 1) * tokens)
                    for o in range(count):
                        rows = jnp.dot(
                            sel_ref[b], token[o][rows_of, :], preferred_element_type=F32
                        ).astype(BF)
                        for e in range(each):
                            held_ref[e, b * CAP : (b + 1) * CAP, o * wide : (o + 1) * wide] = rows[
                                e * CAP : (e + 1) * CAP
                            ]

            rows = jnp.dot(
                self.packing(at_ref[0, expert]), held_ref[expert], preferred_element_type=F32
            ).astype(BF)
            rows_ref[0] = rows
            for i in range(2):
                value = sum(
                    jnp.dot(
                        rows[:, o * wide : (o + 1) * wide],
                        weight[o][0, i],
                        preferred_element_type=F32,
                    )
                    for o in range(count)
                ).astype(BF)
                for q in range(chips):
                    part = value[:, q * own : (q + 1) * own]
                    store_rows(value_ref.at[q], start, used, part, i * own)

        ins = [self.slots_in(), self.select_in()] + [self.whole(part) for part in parts]
        ins += [self.by_expert(piece) for piece in weights]
        ins += [self.whole(array) for array in passed]
        outs = [self.out_by_expert((each, size, count * wide), BF)]
        outs += [self.out_whole((chips, self.room, 2 * own), BF)]
        outs += [self.out_whole(array.shape, BF) for array in (parts[0], *passed)]
        flops = 2 * each * size * count * wide * (2 * self.ff + size)
        scratch = [pltpu.VMEM((each, size, count * wide), BF)]
        zero = jnp.int32(0)
        return self.call(
            kernel, "gate_up", place, zero, wait, each, ins, outs, scratch, flops
        )

    def inner(self, wait, place, chosen, value, base):
        each, own, room, tokens = self.each, self.ff_own, self.room, self.tokens
        steps = 4 if room % 256 == 0 else 3
        size = room // steps
        tile = 64

        def kernel(s_ref, at_ref, sel_ref, chosen_ref, value_ref, base_ref, *refs):
            grads_ref, scaled_ref, table_ref, dots_ref = refs
            step = pl.program_id(0)
            for first in range(0, size, tile):
                rows = slice(first, first + tile)
                gate = value_ref[rows, :own].astype(F32)
                up = value_ref[rows, own:].astype(F32)
                base = base_ref[rows, :].astype(F32)
                chosen = chosen_ref[rows, :]
                sigma = 1.0 / (1.0 + jnp.exp(-gate))
                swish = gate * sigma
                active = swish * up
                grad = chosen * base
                grads_ref[rows, :own] = (
                    grad * up * sigma * (1.0 + gate * (1.0 - sigma))
                ).astype(BF)
                grads_ref[rows, own:] = (grad * swish).astype(BF)
                scaled_ref[rows, :] = (active * chosen).astype(BF)
                dots = jnp.sum(active * base, axis=1, keepdims=True)
                dots_ref[pl.ds(pl.multiple_of(step * size + first, tile), tile), :] = dots

            @pl.when(step == steps - 1)
            def _():
                for e in range(each):
                    start, used = self.extent(s_ref, s_ref[0], e)
                    dots = window(dots_ref, start, self.size).astype(BF)
                    dots = self.unpacked(at_ref[0, e], dots)
                    for b in range(self.ranks):
                        picks = sel_ref[b, e * CAP : (e + 1) * CAP, :].astype(F32)
                        table_ref[e, :, b * tokens : (b + 1) * tokens] = jnp.sum(
                            picks * dots[b * CAP : (b + 1) * CAP], axis=0, keepdims=True
                        )

        by_rows = lambda array: (array, (size, array.shape[1]), lambda c, s: (c, 0))
        ins = [self.slots_in(), self.select_in()]
        ins += [by_rows(array) for array in (chosen, value, base)]
        outs = [
            ((room, cols), BF, (size, cols), lambda c, s: (c, 0)) for cols in (2 * own, own)
        ]
        outs += [self.out_whole((each, 1, self.length), F32)]
        zero = jnp.int32(0)
        scratch = [pltpu.VMEM((room, 1), F32)]
        return self.call(kernel, "inner", place, zero, wait, steps, ins, outs, scratch=scratch)

    def rows_back(self, wait, place, grads, weights):
        each, count, wide, length = self.each, self.count, self.wide, self.length
        chips, tokens, own = len(self.plan.split), self.tokens, self.ff_own

        def kernel(s_ref, at_ref, sel_ref, grads_ref, *refs):
            weight = refs[:count]
            keep_ref, give_ref, held_ref = refs[count:]
            expert = pl.program_id(0)
            start, used = self.extent(s_ref, s_ref[0], expert)
            windows = [window(grads_ref.at[q], start, self.size) for q in range(chips)]
            windows = [
                jnp.concatenate([part[:, i * own : (i + 1) * own] for part in windows], axis=1)
                for i in range(2)
            ]
            rows = [
                sum(
                    lax.dot_general(
                        windows[i],
                        weight[o][0, i],
                        (((1,), (1,)), ((), ())),
                        preferred_element_type=F32,
                    )
                    for i in range(2)
                ).astype(BF)
                for o in range(count)
            ]
            rows = self.unpacked(at_ref[0, expert], jnp.concatenate(rows, axis=1)).astype(BF)
            for b in range(self.ranks):
                held_ref[b, pl.ds(pl.multiple_of(expert * CAP, CAP), CAP), :] = rows[
                    b * CAP : (b + 1) * CAP
                ]

            @pl.when(expert == each - 1)
            def _():
                for b in range(self.ranks):
                    out = jnp.dot(sel_ref[b], held_ref[b], preferred_element_type=F32).astype(BF)
                    keep_ref[b * tokens : (b + 1) * tokens, :] = out[:, :wide]
                    give_ref[b * tokens : (b + 1) * tokens, :] = out[:, wide:]

        ins = [self.slots_in(), self.select_t_in(), self.whole(grads)]
        ins += [self.by_expert(piece) for piece in weights]
        outs = [self.out_whole((length, wide), BF) for _ in range(2)]
        flops = 2 * each * self.size * count * wide * (2 * self.ff + self.size)
        scratch = [pltpu.VMEM((self.ranks, each * CAP, count * wide), BF)]
        zero = jnp.int32(0)
        return self.call(
            kernel, "rows_back", place, zero, wait, each, ins, outs, scratch, flops
        )

    def results(self, wait, place, me, scaled, downs):
        each, width, tokens, size = self.each, self.width, self.tokens, self.size
        half, count, own = self.ranks // 2, self.count, self.ff_own
        cols = min(512, width)

        def kernel(s_ref, at_ref, sel_ref, scaled_ref, *refs):
            down = refs[:count]
            keep_ref, give_ref, slots_ref, held_ref = refs[count:]

            @pl.when(pl.program_id(0) == 0)
            def _():
                for e in range(each):
                    start, used = self.extent(s_ref, s_ref[0], e)
                    value = window(scaled_ref, start, size)
                    slots_ref[e] = self.unpacked(at_ref[0, e], value).astype(BF)

            for e in range(each):
                weight = jnp.concatenate([ref[e, 0] for ref in down], axis=0)
                rows = jnp.dot(slots_ref[e], weight, preferred_element_type=F32).astype(BF)
                for b in range(self.ranks):
                    held_ref[b, e * CAP : (e + 1) * CAP, :] = rows[b * CAP : (b + 1) * CAP]
            for b in range(self.ranks):
                out = jnp.dot(sel_ref[b], held_ref[b], preferred_element_type=F32).astype(BF)
                other = s_ref[1] ^ b
                for side, ref in enumerate((keep_ref, give_ref)):

                    @pl.when(other % 2 == side)
                    def _():
                        ref[other // 2] = out

        ins = [self.slots_in(), self.select_t_in(), self.whole(scaled)]
        ins += [(piece, piece.shape[:3] + (cols,), lambda c, s: (0, 0, 0, c)) for piece in downs]
        out = ((half, tokens, width), BF, (half, tokens, cols), lambda c, s: (0, 0, c))
        outs = [out, out, self.out_whole((each, size, own), BF)]
        flops = 2 * each * size * width * (tokens + own)
        scratch = [pltpu.VMEM((self.ranks, each * CAP, cols), BF)]
        return self.call(
            kernel, "results", place, me, wait, width // cols, ins, outs, scratch, flops
        )

    def down_grads(self, wait, scaled, rows):
        each, count, width, planes = self.each, self.count, self.width, self.planes

        def kernel(s_ref, *refs):
            outs = refs[2 * planes :]
            left = jnp.concatenate([refs[d][0] for d in range(planes)], axis=0).T
            cols = min(512, width)
            for first in range(0, width, cols):
                part = slice(first, first + cols)
                right = jnp.concatenate([refs[planes + d][0, :, part] for d in range(planes)], axis=0)
                total = jnp.dot(left, right, preferred_element_type=F32).astype(BF)
                for o in range(count):
                    outs[o][0, 0, :, part] = total[o * self.ff_wide : (o + 1) * self.ff_wide]

        ins = [self.by_expert(array) for array in (*scaled, *rows)]
        outs = [self.out_by_expert((each, 1, self.ff_wide, width), BF) for _ in range(count)]
        flops = 2 * each * self.size * planes * width * self.ff_own
        zero = jnp.int32(0)
        return self.call(kernel, "down_grads", zero, zero, wait, each, ins, outs, flops=flops)

    def weight_grads(self, wait, places, rows, grads):
        each, count, wide, planes = self.each, self.count, self.wide, self.planes
        own, chips = self.ff_own, len(self.plan.split)
        tiles = 1 if planes * chips * self.room * own < 14 << 20 else chips
        at_once = chips // tiles

        def kernel(s_ref, *refs):
            outs = refs[2 * planes :]
            expert = lax.rem(pl.program_id(0), each)
            starts = [
                self.extent(s_ref, lax.rem(s_ref[0] + planes - d, planes), expert)[0]
                for d in range(planes)
            ]
            left = jnp.concatenate([refs[d][0] for d in range(planes)], axis=0).T
            for q in range(at_once):
                right = jnp.concatenate(
                    [
                        window(refs[planes + d].at[q], starts[d], self.size)
                        for d in range(planes)
                    ],
                    axis=0,
                )
                total = jnp.dot(left, right, preferred_element_type=F32).astype(BF)
                for o in range(count):
                    for i in range(2):
                        outs[o][0, i, :, q * own : (q + 1) * own] = total[
                            o * wide : (o + 1) * wide, i * own : (i + 1) * own
                        ]

        ins = [
            (array, (1,) + array.shape[1:], lambda e, s: (lax.rem(e, each), 0, 0)) for array in rows
        ]
        block = (at_once,) + grads[0].shape[1:]
        ins += [(array, block, lambda e, s: (lax.div(e, each), 0, 0), tiles == 1) for array in grads]
        out = (
            (each, 2, wide, self.ff),
            BF,
            (1, 2, wide, at_once * own),
            lambda e, s: (lax.rem(e, each), 0, 0, lax.div(e, each)),
        )
        outs = [out] * count
        flops = 4 * each * self.size * planes * count * wide * self.ff
        zero = jnp.int32(0)
        return self.call(
            kernel, "weight_grads", places[0], zero, wait, tiles * each, ins, outs, flops=flops
        )


def normed_blocks(near, far, masks, gain, me):
    half, tokens, width = near.shape

    def kernel(s_ref, gain_ref, near_ref, far_ref, x_ref, hidden_ref):
        step = pl.program_id(0)
        for side, ref in enumerate((near_ref, far_ref)):

            @pl.when(step // half == side)
            def _():
                value = ref[0].astype(F32)
                scale = lax.rsqrt(jnp.mean(value * value, axis=-1, keepdims=True) + EPS)
                value = value * scale
                x_ref[...] = value.astype(BF)
                hidden_ref[...] = (value * gain_ref[...]).astype(BF)

    block = pl.BlockSpec((tokens, width), lambda n, s: (s[0] ^ s[1 + n], 0))
    shape = jax.ShapeDtypeStruct((2 * half * tokens, width), BF)
    order = list(masks) + [mask ^ 1 for mask in masks]
    return pl.pallas_call(
        kernel,
        grid_spec=pltpu.PrefetchScalarGridSpec(
            num_scalar_prefetch=1,
            grid=(2 * half,),
            in_specs=[
                pl.BlockSpec((1, width), lambda n, s: (0, 0)),
                pl.BlockSpec((1, tokens, width), lambda n, s: (jnp.minimum(n, half - 1), 0, 0)),
                pl.BlockSpec((1, tokens, width), lambda n, s: (jnp.maximum(n - half, 0), 0, 0)),
            ],
            out_specs=[block, block],
        ),
        out_shape=[shape, shape],
        compiler_params=pltpu.CompilerParams(vmem_limit_bytes=32 << 20),
        cost_estimate=pl.CostEstimate(
            flops=0, bytes_accessed=12 * half * tokens * width, transcendentals=0
        ),
        name="normed_blocks",
    )(jnp.concatenate([me[None], jnp.array(order, jnp.int32)]), gain.reshape(1, width), near, far)


def local(
    layer_in,
    cotangent,
    file_lengths,
    routes,
    attn_gain,
    q_gain,
    k_gain,
    ffn_gain,
    w_q,
    w_k,
    w_v,
    w_o,
    router,
    expert_gate,
    expert_up,
    expert_down,
):
    planes = lax.axis_size("seq")
    ranks = lax.axis_size("ctx")
    plane = lax.axis_index("seq")
    me = lax.axis_index("ctx")
    nbits = ranks.bit_length() - 1
    tokens, width = layer_in.shape[1:]
    length = tokens * ranks
    total_tokens = length * planes
    blocks = planes * ranks
    wide = width // ranks
    heads = wide // HEAD_DIM
    experts = router.shape[1]
    per_plane = expert_gate.shape[0]
    ff = expert_gate.shape[2]
    ff_wide = ff // ranks
    scale = HEAD_DIM ** (-0.5)

    split_bits = list(range(1, nbits))
    plan = Plan(0, split_bits[::-1], [0], per_plane, me)
    plans = [plan]
    each, pieces = plan.each, plan.count
    ff_own = ff // len(plan.split)

    small = [routes[0].T.astype(BF), router.T, jnp.stack([attn_gain, q_gain, k_gain, ffn_gain])]
    small_own = jnp.concatenate([part.reshape(-1) for part in small])
    small_all = lax.all_gather(small_own, "ctx")
    small_all = lax.all_gather(small_all, "seq").reshape(blocks, -1)
    packed_gate_up = pack([expert_gate, expert_up], plans, ff_wide, ranks)
    packed_down = pack([expert_down], plans, 0, ranks)
    w_own = jnp.stack([w_q, w_k, w_v, w_o])
    rows_own = w_own.shape[1]
    w_ctx = lax.all_to_all(
        jnp.transpose(w_own.reshape(4, rows_own, ranks, wide), (2, 0, 1, 3)),
        "ctx",
        split_axis=0,
        concat_axis=0,
        tiled=True,
    )

    masks = list(range(0, ranks, 2))
    first_sent = mark(w_ctx, small_all)
    x_sent = held(layer_in[0], first_sent)
    x_parts = [x_sent if mask == 0 else swap(x_sent, mask) for mask in masks]
    x_near = jnp.stack(x_parts)
    cot_sent = held(cotangent[0], mark(x_parts[1]))
    cot_parts = [cot_sent if mask == 0 else swap(cot_sent, mask) for mask in masks]
    x_far = swap(x_near, 1)

    def gather_masks(value):
        near = jnp.stack([value if mask == 0 else swap(value, mask) for mask in masks])
        return near, swap(near, 1)

    def sum_masks(near, far):
        total = near.astype(F32) + swap(far, 1).astype(F32)
        out = total[0]
        for number in range(1, len(masks)):
            out = out + swap(total[number].astype(BF), masks[number]).astype(F32)
        return out

    def by_rows(part):
        part = lax.all_gather(part, "seq", axis=0, tiled=False)
        return jnp.transpose(part, (2, 0, 1, 3, 4)).reshape(-1, width, wide)

    w_all = by_rows(w_ctx)
    w_qkv = w_all[:3]
    w_out = w_all[3].reshape(ranks, wide, wide)
    near_order = me ^ jnp.array(masks, jnp.int32)
    w_near, w_far = jnp.take(w_out, near_order, axis=0), jnp.take(w_out, near_order ^ 1, axis=0)
    ends = np.cumsum([part.size for part in small])
    routes_all = small_all[:, : ends[0]].reshape(blocks, -1, tokens).astype(jnp.int32)
    router_all = small_all[:, ends[0] : ends[1]].reshape(blocks, experts, -1)
    router_all = jnp.transpose(router_all, (0, 2, 1)).reshape(width, experts)
    gains = small_all[:, ends[1] :].reshape(blocks, 4, -1)
    gains = jnp.transpose(gains, (1, 0, 2)).reshape(4, width).astype(F32)
    gain_attn = gains[0] + mark(packed_down[0])
    own_gains = lax.dynamic_slice_in_dim(gains, me * wide, wide, 1)
    router_own = lax.dynamic_slice_in_dim(router_all, me * wide, wide, 0)
    gain_query, gain_key, gain_ffn = own_gains[1], own_gains[2], own_gains[3]
    x_normed, hidden = normed_blocks(x_near, x_far, masks, gain_attn, me)

    def own_columns(near, far):
        sides = [lax.dynamic_slice_in_dim(side, me * wide, wide, 2) for side in (near, far)]
        both = jnp.stack(sides, axis=1).reshape(ranks, tokens, wide)
        both = jnp.take(both, me ^ jnp.arange(ranks, dtype=jnp.int32), axis=0)
        return both.reshape(length, wide).astype(F32)

    sent_gate_up = send_pieces(packed_gate_up, plans)
    sent_down = send_pieces(packed_down, plans)

    size = ranks * CAP
    lower = jnp.triu(jnp.ones((tokens, tokens), BF), 1)
    own_experts = plane * per_plane + plan.experts[:each]
    named = jnp.any(routes_all[:, None] == own_experts[None, :, None, None], axis=2)
    rank = mm("bet,tu->beu", named.astype(BF), lower)
    slot_numbers = jnp.arange(CAP, dtype=jnp.int32)
    select = named[:, :, None, :] & (rank[:, :, None, :] == slot_numbers[None, None, :, None])
    select = select.astype(BF).reshape(blocks, each * CAP, tokens)
    select_t = jnp.transpose(select, (0, 2, 1))
    in_block = jnp.sum(named.astype(jnp.int32), axis=2).reshape(planes, ranks, each)
    before = jnp.cumsum(in_block, axis=1) - in_block
    slot_at = jnp.where(
        slot_numbers < in_block[..., None], before[..., None] + slot_numbers, -1
    )
    slot_at = jnp.transpose(slot_at, (0, 2, 1, 3)).reshape(planes, each, 1, size)
    used = jnp.sum(in_block, axis=1)
    padded = (used + 15) // 16 * 16
    starts = jnp.cumsum(padded, axis=1) - padded
    layout = (
        jnp.concatenate([starts, used], axis=1).reshape(-1),
        slot_at,
        select,
        select_t,
    )

    expert_ids = jnp.arange(experts, dtype=jnp.int32)
    counts_all = jnp.sum(
        (routes_all.reshape(blocks, 1, -1) == expert_ids[None, :, None]).astype(jnp.int32), axis=2
    )

    places = [lax.rem(plane + planes - offset, planes) for offset in range(planes)]

    by_chunk = jnp.sum(counts_all.reshape(planes, ranks, experts), axis=1)
    by_chunk = jnp.sum(((by_chunk + 15) // 16 * 16).reshape(planes, -1, each), axis=2)
    room_full = each * size + 64
    room_few = each * size * 3 // 4
    fits = jnp.max(by_chunk) <= room_few - 64

    cot_near = held(jnp.stack(cot_parts), mark(w_qkv))
    query_lin = mm("td,de->te", hidden, w_qkv[0])
    key_lin = mm("td,de->te", hidden, w_qkv[1])
    value_lin = mm("td,de->te", hidden, w_qkv[2])
    squares = jnp.stack([jnp.sum(query_lin * query_lin, -1), jnp.sum(key_lin * key_lin, -1)])
    squares = jnp.sum(lax.all_gather(squares, "ctx"), axis=0) / width
    query_scale, key_scale = lax.rsqrt(squares + EPS)[:, :, None]
    positions = jnp.arange(length, dtype=jnp.int32)
    cosine, sine = angles(positions)

    def by_head(value):
        return value.reshape(length, heads, HEAD_DIM)

    queries = rotate(by_head(query_lin * query_scale * gain_query), cosine, sine).astype(BF)
    keys = rotate(by_head(key_lin * key_scale * gain_key), cosine, sine).astype(BF)
    values = by_head(value_lin.astype(BF))
    lengths = file_lengths[0]
    files = segments(jnp.cumsum(lengths) - lengths, positions)
    allowed = (positions[None, :] <= positions[:, None]) & (files[None, :] == files[:, None])
    scores = mm("qhd,khd->hqk", queries, keys) * scale
    scores = jnp.where(allowed[None], scores, NEG)
    shifted = jnp.exp(scores - jnp.max(scores, axis=-1, keepdims=True))
    weights = (shifted / jnp.sum(shifted, axis=-1, keepdims=True)).astype(BF)
    attended = mm("hqk,khd->qhd", weights, values)
    mixed = (attended.reshape(length, wide) + mark(*cot_parts[1:])).astype(BF)
    mixed_near, mixed_far = gather_masks(mixed)
    own_inputs = own_columns(x_near, x_far)
    resid = own_inputs + mm("cld,cde->le", mixed_near, w_near) + mm("cld,cde->le", mixed_far, w_far)

    ffn_square = jnp.sum(resid * resid, -1)
    ffn_square = jnp.sum(lax.all_gather(ffn_square, "ctx"), axis=0) / width
    ffn_scale = lax.rsqrt(ffn_square + EPS)[:, None]
    normed = (resid * ffn_scale * gain_ffn).astype(BF)
    logits = mm("td,de->et", normed, router_own)
    for bit in range(nbits):
        logits = logits + swap(logits, 1 << bit)
    shifted = jnp.exp(logits - jnp.max(logits, axis=0, keepdims=True))
    probs_t = shifted / jnp.sum(shifted, axis=0, keepdims=True)
    probs = probs_t.T

    cot_far = swap(cot_near, 1)
    own_cot = own_columns(cot_near, cot_far)

    order_back = list(range(1, planes)) + [0]
    same_core = [list(range(core, ranks, 2)) for core in range(2)]

    def exchange_table(table):
        came = jnp.stack([to_earlier(table[d], d) for d in range(planes)])[None]
        for bit in range(nbits):
            came = jnp.concatenate([came, swap(came, 1 << bit)])
        came = jnp.take(came, me ^ jnp.arange(ranks, dtype=jnp.int32), axis=0)
        came = jnp.sum(came.reshape((ranks // 2, 2) + came.shape[1:]), axis=0)
        came = jnp.transpose(came, (1, 0, 2, 3)).reshape(planes, -1, length)
        turn = lax.rem(jnp.arange(planes, dtype=jnp.int32) + planes - plane, planes)
        return jnp.take(came, turn, axis=0).reshape(experts, length).T

    def run_experts(room):
        ops = Experts(plan, ranks, tokens, wide, ff, width, planes, room, layout)
        rows, cot_rows, terms, hidden_grads, scaled, at_slots = [], [], [], [], [], []
        table, back, lead_passed, probs_kept, cot_passed = [], {}, [normed], [], []
        sums = []

        def start_chunk(offset, wait):
            lead = lead_passed[-1] if offset == 0 else shift(lead_passed[-1])
            probs_kept.append(probs_t if offset == 0 else shift(probs_kept[-1]))
            near = []
            if offset:
                near = [cot_near if offset == 1 else shift(cot_passed[-1])]
            found, value, *passed = ops.gate_up(
                [wait], places[offset], [lead, swap(lead, 1)], sent_gate_up, near
            )
            rows.append(found)
            lead_passed.append(passed[0])
            cot_passed.extend(passed[1:])
            terms.append(
                lax.psum_scatter(
                    value, "ctx", scatter_dimension=0, axis_index_groups=same_core, tiled=False
                )
            )
            return found

        def middle_chunk(offset, wait):
            near = cot_passed[offset] if offset < planes - 1 else shift(cot_passed[-1])
            far = cot_far if offset == 0 else swap(near, 1)
            own_probs = jnp.take(probs_kept[offset], own_experts, axis=0)
            found, base, chosen = ops.cot_rows(
                [wait], places[offset], me, own_probs, near, far, masks, sent_down
            )
            cot_rows.append(found)
            grads, active, part = ops.inner([found], places[offset], chosen, terms[offset], base)
            hidden_grads.append(
                lax.all_gather(grads, "ctx", axis=0, axis_index_groups=same_core)
            )
            scaled.append(active)
            table.append(part.reshape(each, length))
            return active

        def end_chunk(offset, wait):
            keep, give = ops.rows_back(
                [wait], places[offset], hidden_grads[offset], sent_gate_up
            )
            back[offset] = keep.astype(F32) + swap(give, 1).astype(F32)
            return keep

        def finish_chunk(offset, wait):
            keep, give, found = ops.results(
                [wait], places[offset], me, scaled[offset], sent_down
            )
            at_slots.append(found)
            both = (keep.astype(F32) + swap(give, 1).astype(F32)).astype(BF)
            sums.append(both)
            return keep

        wait = start_chunk(0, normed)
        for offset in range(1, planes):
            wait = start_chunk(offset, wait)
            wait = middle_chunk(offset - 1, wait)
            wait = finish_chunk(offset - 1, wait)
            if offset >= 2:
                wait = end_chunk(offset - 2, wait)
        wait = middle_chunk(planes - 1, wait)
        wait = finish_chunk(planes - 1, wait)
        wait = end_chunk(planes - 2, wait)
        down_parts = ops.down_grads([wait], at_slots, cot_rows)
        wait = end_chunk(planes - 1, down_parts[0])
        gate_up_parts = ops.weight_grads([wait], places, rows, hidden_grads)
        total = sums[1]
        for offset in order_back[1:]:
            total = shift(total).astype(F32) + sums[offset].astype(F32)
            total = total.astype(BF)
        carry = back[1]
        for offset in order_back[1:]:
            carry = shift(carry.astype(BF)).astype(F32) + back[offset]
        return carry, total, exchange_table(table), down_parts, gate_up_parts

    grad_normed, out_sum, grad_probs, down_parts, gate_up_parts = lax.cond(
        fits, lambda: run_experts(room_few), lambda: run_experts(room_full)
    )

    grad_logits = (
        probs * (grad_probs - jnp.sum(probs * grad_probs, axis=-1, keepdims=True))
    ).astype(BF)
    grad_router = mm("td,te->de", normed, grad_logits)
    grad_normed = grad_normed + mm("te,de->td", grad_logits, router_own)

    down_parts = send_pieces(down_parts, plans)
    gate_up_parts = send_pieces(gate_up_parts, plans)

    def to_plane(part):
        size = part.shape[-2] // planes
        own = [lax.dynamic_slice_in_dim(part, p * size, size, part.ndim - 2) for p in places]
        carry = own[1]
        for offset in order_back[1:]:
            carry = shift(carry).astype(F32) + own[offset].astype(F32)
            carry = carry.astype(part.dtype)
        return carry

    def norm_back(values, own_scale, gain, grad, inner):
        return own_scale * gain * grad - values * (own_scale * own_scale * own_scale) * inner

    inner = jnp.sum(resid * gain_ffn * grad_normed, -1)
    inner = jnp.sum(lax.all_gather(inner, "ctx"), axis=0)
    grad_ffn_gain = jnp.sum(grad_normed * resid * ffn_scale, axis=0)
    grad_resid = own_cot + norm_back(resid, ffn_scale, gain_ffn, grad_normed, inner[:, None] / width)
    grad_attn = grad_resid.astype(BF)
    both = jnp.stack([resid, grad_resid]).reshape(2, ranks, tokens, wide).transpose(1, 0, 2, 3)
    both = lax.all_to_all(both, "ctx", split_axis=0, concat_axis=0, tiled=True)
    resid_own, grad_resid_own = jnp.transpose(both, (1, 2, 0, 3)).reshape(2, tokens, width)

    mixed_grads = [mm("le,cde->cld", grad_attn, side).astype(BF) for side in (w_near, w_far)]
    share_down = unpack(down_parts, plans, 0, ranks, [mixed_grads[0]])[0]
    share_gate, share_up = unpack(gate_up_parts, plans, ff_wide, ranks, [mixed_grads[0]])
    grad_mixed = sum_masks(*mixed_grads) + mark(share_down, share_gate, share_up)
    grad_mixed = grad_mixed.astype(BF)
    grad_heads = by_head(grad_mixed)
    grad_weights = mm("qhd,khd->hqk", grad_heads, values)
    delta = jnp.sum(grad_heads.astype(F32) * attended, axis=-1).transpose(1, 0)[:, :, None]
    grad_scores = (weights.astype(F32) * (grad_weights - delta)).astype(BF)
    grad_query = mm("hqk,khd->qhd", grad_scores, keys) * scale
    grad_key = mm("hqk,qhd->khd", grad_scores, queries) * scale
    grad_value = mm("hqk,qhd->khd", weights, grad_heads).reshape(length, wide).astype(BF)
    grad_query = rotate(grad_query, cosine, -sine).reshape(length, wide)
    grad_key = rotate(grad_key, cosine, -sine).reshape(length, wide)
    inners = jnp.stack(
        [
            jnp.sum(query_lin * gain_query * grad_query, -1),
            jnp.sum(key_lin * gain_key * grad_key, -1),
        ]
    )
    inners = jnp.sum(lax.all_gather(inners, "ctx"), axis=0)[:, :, None] / width
    grad_query_gain = jnp.sum(grad_query * query_lin * query_scale, axis=0)
    grad_key_gain = jnp.sum(grad_key * key_lin * key_scale, axis=0)
    grad_query_b = norm_back(query_lin, query_scale, gain_query, grad_query, inners[0]).astype(BF)
    grad_key_b = norm_back(key_lin, key_scale, gain_key, grad_key, inners[1]).astype(BF)
    grads = (grad_query_b, grad_key_b, grad_value)
    grad_hidden = sum(mm("te,de->td", grads[i], w_qkv[i]) for i in range(3))
    grad_attn_gain = jnp.sum(grad_hidden * x_normed.astype(F32), axis=0)
    grad_hidden = grad_hidden.astype(BF).reshape(ranks, tokens, width)
    grad_hidden = sum_masks(
        jnp.take(grad_hidden, near_order, axis=0), jnp.take(grad_hidden, near_order ^ 1, axis=0)
    )
    out_sum = out_sum.astype(F32) + mark(inners)
    out_blocks = [
        swap(out_sum[place_of].astype(BF), mask) for place_of, mask in enumerate(masks) if mask
    ]
    grad_out_w = [mm("cld,le->cde", side, grad_attn) for side in (mixed_near, mixed_far)]
    grad_out_w = jnp.stack(grad_out_w, axis=1).reshape(ranks, wide, wide)
    grad_out_w = jnp.take(grad_out_w, me ^ jnp.arange(ranks, dtype=jnp.int32), axis=0)
    grad_out_w = grad_out_w.reshape(width, wide)
    weight_grads = [mm("td,te->de", hidden, grad).astype(BF) for grad in grads]
    weight_grads = [
        to_plane(jnp.stack(weight_grads[:2])),
        to_plane(jnp.stack([weight_grads[2], grad_out_w.astype(BF)])),
    ]
    weight_grads = jnp.concatenate(weight_grads)
    weight_grads = weight_grads.reshape(4, ranks, rows_own, wide).transpose(1, 0, 2, 3)
    weight_grads = lax.all_to_all(weight_grads, "ctx", split_axis=0, concat_axis=0, tiled=True)
    weight_grads = weight_grads.transpose(1, 2, 0, 3).reshape(4, rows_own, width).astype(F32)

    own_x = layer_in[0].astype(F32)
    own_scale = lax.rsqrt(jnp.mean(own_x * own_x, axis=-1, keepdims=True) + EPS)
    inner = jnp.mean(own_x * gain_attn * grad_hidden, axis=-1, keepdims=True)
    grad_input = grad_resid_own + norm_back(own_x, own_scale, gain_attn, grad_hidden, inner)

    own_small = jnp.concatenate(
        [grad_router, jnp.stack([grad_query_gain, grad_key_gain, grad_ffn_gain], axis=1)], axis=1
    )
    small_grads = jnp.zeros((experts + 3, width), F32)
    small_grads = lax.dynamic_update_slice_in_dim(small_grads, own_small.T, me * wide, 1)
    small_grads = jnp.concatenate([small_grads, grad_attn_gain[None]], axis=0)
    small_grads = small_grads.reshape(experts + 4, planes, -1).transpose(1, 0, 2)
    parts_of = [pick(small_grads, p, 0) for p in places]
    carry = parts_of[1]
    for offset in order_back[1:]:
        carry = shift(carry) + parts_of[offset]
    carry = carry.reshape(experts + 4, ranks, -1).transpose(1, 0, 2)
    carry = lax.all_to_all(carry, "ctx", split_axis=0, concat_axis=0, tiled=True)
    small_grads = jnp.sum(carry, axis=0).T

    out_own = out_sum[0] + sum(block.astype(F32) for block in out_blocks)
    output = resid_own + out_own
    return (
        output.astype(BF)[None],
        grad_input.astype(BF)[None],
        small_grads[:, experts + 3],
        small_grads[:, experts],
        small_grads[:, experts + 1],
        small_grads[:, experts + 2],
        weight_grads[0],
        weight_grads[1],
        weight_grads[2],
        weight_grads[3],
        small_grads[:, :experts],
        share_gate,
        share_up,
        share_down,
        counts_all,
    )


def solution(mesh):
    tokens = P("seq", "ctx", None)
    flat = P(BOTH)
    rows = P(BOTH, None)
    return jax.shard_map(
        local,
        mesh=mesh,
        in_specs=(tokens, tokens, P("seq", None), tokens)
        + (flat,) * 4
        + (rows,) * 5
        + (tokens,) * 3,
        out_specs=(tokens, tokens) + (flat,) * 4 + (rows,) * 5 + (tokens,) * 3 + (P(),),
        check_vma=False,
    )
```

```python
import jax
import jax.numpy as jnp
import numpy as np
from jax import lax
from jax.experimental import pallas as pl
from jax.experimental.pallas import tpu as pltpu
from jax.sharding import PartitionSpec as P

HEAD_DIM = 128
CAP = 32
EPS = 1e-05
NEG = -1e30
BF = jnp.bfloat16
F32 = jnp.float32
BOTH = ("seq", "ctx")


def mm(spec, a, b):
    return jnp.einsum(spec, a, b, preferred_element_type=F32)


def angles(positions):
    half = HEAD_DIM // 2
    inverse = 10000.0 ** (-(jnp.arange(half, dtype=F32) * 2.0 / HEAD_DIM))
    theta = positions.astype(F32)[:, None] * inverse[None, :]
    return (jnp.cos(theta)[:, None, :], jnp.sin(theta)[:, None, :])


def rotate(values, cosine, sine):
    half = values.shape[-1] // 2
    first = values[..., :half]
    second = values[..., half:]
    return jnp.concatenate(
        [first * cosine - second * sine, second * cosine + first * sine], axis=-1
    )


def segments(offsets, positions):
    return jnp.sum((positions[:, None] >= offsets[None, :]).astype(jnp.int32), axis=1) - 1


def swap(value, mask):
    size = lax.axis_size("ctx")
    return lax.ppermute(value, "ctx", [(i, i ^ mask) for i in range(size)])


def shift(value):
    size = lax.axis_size("seq")
    return lax.ppermute(value, "seq", [(i, (i + 1) % size) for i in range(size)])


def to_earlier(value, offset):
    size = lax.axis_size("seq")
    if offset % size == 0:
        return value
    return lax.ppermute(value, "seq", [(i, (i - offset) % size) for i in range(size)])


def subsets(bits):
    out = []
    for number in range(1 << len(bits)):
        mask = 0
        for place, bit in enumerate(reversed(bits)):
            mask |= (number >> place & 1) << bit
        out.append(mask)
    return out


def coordinate(index, bits):
    out = jnp.int32(0)
    for bit in bits:
        out = out * 2 + (lax.shift_right_logical(index, bit) & 1)
    return out


def mark(*arrays):
    return sum(array[(0,) * array.ndim].astype(F32) * 0.0 for array in arrays)


def pick(value, index, axis):
    return lax.dynamic_index_in_dim(value, index, axis, keepdims=False)


def held(value, zero):
    return value + zero.astype(value.dtype)


class Plan:
    def __init__(self, split, shared, expert_at, me):
        self.split = subsets(split)
        self.masks = subsets(shared)
        self.count = len(self.masks)
        self.each = expert_at.shape[0] // self.count
        place = coordinate(me, shared)
        self.experts = jnp.concatenate(
            [
                lax.dynamic_slice_in_dim(expert_at, (place ^ o) * self.each, self.each, 0)
                for o in range(self.count)
            ]
        )
        self.others = jnp.concatenate(
            [jnp.full((self.each,), me ^ self.masks[o], jnp.int32) for o in range(self.count)]
        )


def exchange_blocks(value, other, block):
    parts = [value[:, i * block : (i + 1) * block] for i in range(value.shape[1] // block)]
    turned = jnp.concatenate([parts[i ^ 1] for i in range(len(parts))], axis=1)
    return jnp.where(other & 1 == 1, turned, value)


def take_blocks(part, order):
    count = order.shape[0]
    blocks = part.reshape(part.shape[:-1] + (count, part.shape[-1] // count))
    return jnp.take(blocks, order, axis=-2).reshape(part.shape)


def pack(arrays, plans, block, ranks):
    total = len(arrays)
    rows, cols = arrays[0].shape[1:]
    each, count = plans[0].each, plans[0].count
    pieces = len(plans) * count
    experts = jnp.concatenate([plan.experts for plan in plans])
    others = jnp.concatenate([plan.others for plan in plans])
    if block % 128:
        out = []
        for number in range(pieces):
            few = experts[number * each : (number + 1) * each]
            part = jnp.stack([array[few] for array in arrays], axis=1)
            order = jnp.arange(ranks, dtype=jnp.int32) ^ (others[number * each] & 1)
            out.append(take_blocks(part, order))
        return out

    def kernel(experts_ref, others_ref, *refs):
        step = pl.program_id(0)
        for i in range(total):
            value = refs[i][0]
            if block:
                value = exchange_blocks(value, others_ref[step], block)
            for number in range(pieces):

                @pl.when(step // each == number)
                def _():
                    refs[total + number][0, i] = value

    def out_spec(number):
        return pl.BlockSpec(
            (1, total, rows, cols),
            lambda step, e, t: (jnp.clip(step - number * each, 0, each - 1), 0, 0, 0),
        )

    return pl.pallas_call(
        kernel,
        grid_spec=pltpu.PrefetchScalarGridSpec(
            num_scalar_prefetch=2,
            grid=(pieces * each,),
            in_specs=[pl.BlockSpec((1, rows, cols), lambda step, e, t: (e[step], 0, 0))] * total,
            out_specs=[out_spec(number) for number in range(pieces)],
        ),
        out_shape=[jax.ShapeDtypeStruct((each, total, rows, cols), BF)] * pieces,
        compiler_params=pltpu.CompilerParams(vmem_limit_bytes=48 << 20),
        cost_estimate=pl.CostEstimate(
            flops=0, bytes_accessed=4 * total * arrays[0].size, transcendentals=0
        ),
        name="pack",
    )(experts, others, *arrays)


def unpack(parts, plans, block, ranks, wait):
    each, total, rows, cols = parts[0].shape
    count = plans[0].count
    pieces = len(parts)
    experts = jnp.concatenate([plan.experts for plan in plans])
    others = jnp.concatenate([plan.others for plan in plans])
    if block % 128:
        out = [jnp.zeros((pieces * each, rows, cols), F32)] * total
        for number in range(pieces):
            order = jnp.arange(ranks, dtype=jnp.int32) ^ (others[number * each] & 1)
            part = take_blocks(parts[number], order).astype(F32)
            out = [
                lax.dynamic_update_slice_in_dim(out[i], part[:, i], experts[number * each], 0)
                for i in range(total)
            ]
        return out

    def kernel(experts_ref, others_ref, *refs):
        step = pl.program_id(0)
        for number in range(pieces):

            @pl.when(step // each == number)
            def _():
                for i in range(total):
                    value = refs[number][0, i]
                    if block:
                        value = exchange_blocks(value, others_ref[step], block)
                    refs[pieces + len(wait) + i][0] = value.astype(F32)

    def in_spec(number):
        return pl.BlockSpec(
            (1, total, rows, cols),
            lambda step, e, t: (jnp.clip(step - number * each, 0, each - 1), 0, 0, 0),
        )

    return pl.pallas_call(
        kernel,
        grid_spec=pltpu.PrefetchScalarGridSpec(
            num_scalar_prefetch=2,
            grid=(pieces * each,),
            in_specs=[in_spec(number) for number in range(pieces)]
            + [pl.BlockSpec(memory_space=pl.ANY)] * len(wait),
            out_specs=[pl.BlockSpec((1, rows, cols), lambda step, e, t: (e[step], 0, 0))] * total,
        ),
        out_shape=[jax.ShapeDtypeStruct((pieces * each, rows, cols), F32)] * total,
        compiler_params=pltpu.CompilerParams(vmem_limit_bytes=48 << 20),
        cost_estimate=pl.CostEstimate(
            flops=0, bytes_accessed=6 * total * pieces * each * rows * cols, transcendentals=0
        ),
        name="unpack",
    )(experts, others, *parts, *wait)


def send_piece(part, number, plans):
    count = plans[0].count
    mask = plans[number // count].masks[number % count]
    return swap(part, mask) if mask else part


def send_pieces(parts, plans):
    return [send_piece(part, number, plans) for number, part in enumerate(parts)]


def window(ref, start, size):
    last = ref.shape[0] - 64
    return jnp.concatenate(
        [
            ref[pl.ds(pl.multiple_of(jnp.minimum(start + i, last), 16), 64), :]
            for i in range(0, size, 64)
        ],
        axis=0,
    )


def store_rows(ref, start, used, value, first=0):
    for i in range(0, value.shape[0], 64):

        @pl.when(used > i)
        def _():
            rows = pl.ds(pl.multiple_of(start + i, 16), 64)
            ref[rows, first : first + value.shape[1]] = value[i : i + 64].astype(ref.dtype)


class Experts:
    def __init__(self, plan, ranks, tokens, wide, ff, width, planes, room, layout):
        self.plan, self.ranks, self.tokens, self.wide = plan, ranks, tokens, wide
        self.ff, self.width, self.planes, self.room = ff, width, planes, room
        self.each, self.count = plan.each, plan.count
        self.ff_own = ff // len(plan.split)
        self.ff_wide = ff // ranks
        self.size = ranks * CAP
        self.length = ranks * tokens
        self.scalars, self.slot_at, self.select, self.select_t = layout

    def call(self, kernel, name, place, me, wait, grid, ins, outs, scratch=(), flops=0):
        arrays = [entry[0] for entry in ins]
        size = sum(array.size * array.dtype.itemsize for array in arrays)
        size += sum(int(np.prod(shape)) * jnp.dtype(kind).itemsize for shape, kind, _, _ in outs)
        first, last = len(ins) + 1, len(ins) + 1 + len(wait)

        def body(*refs):
            kernel(*refs[:first], *refs[last:])

        def in_spec(block, index, once=False):
            if once:
                return pl.BlockSpec(block, index, pipeline_mode=pl.Buffered(1))
            return pl.BlockSpec(block, index)

        return pl.pallas_call(
            body,
            grid_spec=pltpu.PrefetchScalarGridSpec(
                num_scalar_prefetch=1,
                grid=(grid,),
                in_specs=[in_spec(*entry[1:]) for entry in ins]
                + [pl.BlockSpec(memory_space=pl.ANY)] * len(wait),
                out_specs=[pl.BlockSpec(block, index) for _, _, block, index in outs],
                scratch_shapes=list(scratch),
            ),
            out_shape=[jax.ShapeDtypeStruct(shape, kind) for shape, kind, _, _ in outs],
            compiler_params=pltpu.CompilerParams(vmem_limit_bytes=58 << 20),
            cost_estimate=pl.CostEstimate(flops=flops, bytes_accessed=size, transcendentals=0),
            name=name,
        )(jnp.concatenate([jnp.stack([place, me]), self.scalars]), *arrays, *wait)

    def extent(self, s_ref, place, expert):
        base = 2 + place * 2 * self.each + expert
        return s_ref[base], s_ref[base + self.each]

    def slots_in(self):
        block = (1,) + self.slot_at.shape[1:]
        return (self.slot_at, block, lambda e, s: (s[0], 0, 0, 0), True)

    def select_in(self):
        block = (self.ranks,) + self.select.shape[1:]
        return (self.select, block, lambda e, s: (s[0], 0, 0), True)

    def select_t_in(self):
        block = (self.ranks,) + self.select_t.shape[1:]
        return (self.select_t, block, lambda e, s: (s[0], 0, 0), True)

    def by_expert(self, array):
        block = (1,) + array.shape[1:]
        return (array, block, lambda e, s: (e,) + (0,) * (len(block) - 1))

    def whole(self, array, once=True):
        return (array, array.shape, lambda e, s: (0,) * array.ndim, once)

    def out_by_expert(self, shape, kind):
        block = (1,) + shape[1:]
        return (shape, kind, block, lambda e, s: (e,) + (0,) * (len(block) - 1))

    def out_whole(self, shape, kind):
        return (shape, kind, shape, lambda e, s: (0,) * len(shape))

    def packed(self, columns, kind=BF):
        return self.out_whole((self.room, columns), kind)

    def packing(self, at):
        rows = lax.broadcasted_iota(jnp.int32, (self.size, self.size), 0)
        return jnp.where(rows == at, 1.0, 0.0).astype(BF)

    def unpacked(self, at, value):
        return lax.dot_general(
            self.packing(at), value, (((0,), (0,)), ((), ())), preferred_element_type=F32
        )

    def weight_of(self, refs, i):
        return jnp.concatenate([ref[0, i] for ref in refs], axis=0)

    def cot_rows(self, wait, place, me, probs, near, far, masks, downs):
        each, count, width, tokens = self.each, self.count, self.width, self.tokens
        half, own, size = len(masks), self.ff_own, self.size
        cols = min(512, width)

        def kernel(s_ref, at_ref, sel_ref, probs_ref, near_ref, far_ref, *refs):
            down = refs[:count]
            rows_ref, base_ref, packed_ref, held_ref, sum_ref = refs[count:]
            step = pl.program_id(0)

            for number, mask in enumerate(masks):
                for side, ref in enumerate((near_ref, far_ref)):
                    held_ref[s_ref[1] ^ mask ^ side] = ref[0, number]
            for b in range(self.ranks):
                rows = jnp.dot(sel_ref[b], held_ref[b], preferred_element_type=F32).astype(BF)
                for e in range(each):
                    rows_ref[e, b * CAP : (b + 1) * CAP, :] = rows[e * CAP : (e + 1) * CAP]
            for e in range(each):
                weight = jnp.concatenate([ref[e, 0] for ref in down], axis=0)
                base = lax.dot_general(
                    rows_ref[e], weight, (((1,), (1,)), ((), ())), preferred_element_type=F32
                )

                @pl.when(step == 0)
                def _():
                    sum_ref[e] = base

                @pl.when(step > 0)
                def _():
                    sum_ref[e] += base

            @pl.when(step == width // cols - 1)
            def _():
                base_ref[...] = jnp.zeros_like(base_ref)
                packed_ref[...] = jnp.zeros_like(packed_ref)
                for e in range(each):
                    start, used = self.extent(s_ref, s_ref[0], e)
                    packing = self.packing(at_ref[0, e])
                    base = jnp.dot(packing, sum_ref[e].astype(BF), preferred_element_type=F32)
                    store_rows(base_ref, start, used, base.astype(BF))
                    chosen = [
                        jnp.sum(
                            sel_ref[b, e * CAP : (e + 1) * CAP, :].astype(F32)
                            * probs_ref[e : e + 1, b * tokens : (b + 1) * tokens],
                            axis=1,
                            keepdims=True,
                        )
                        for b in range(self.ranks)
                    ]
                    chosen = jnp.concatenate(chosen, axis=0).astype(BF)
                    chosen = jnp.dot(packing, chosen, preferred_element_type=F32)
                    store_rows(packed_ref, start, used, chosen)

        by_column = lambda c, s: (0, 0, c)
        ins = [self.slots_in(), self.select_in(), self.whole(probs)]
        of_plane = lambda c, s: (s[0], 0, 0, c)
        ins += [(array, (1, half, tokens, cols), of_plane) for array in (near, far)]
        ins += [(piece, piece.shape[:3] + (cols,), lambda c, s: (0, 0, 0, c)) for piece in downs]
        outs = [
            ((each, size, width), BF, (each, size, cols), by_column),
            self.packed(own),
            self.packed(1, F32),
        ]
        flops = 2 * each * size * width * (tokens + own)
        scratch = [
            pltpu.VMEM((self.ranks, tokens, cols), BF),
            pltpu.VMEM((each, size, own), F32),
        ]
        return self.call(
            kernel, "cot_rows", place, me, wait, width // cols, ins, outs, scratch, flops
        )

    def gate_up(self, wait, place, parts, weights, passed=()):
        each, count, wide, own, size = self.each, self.count, self.wide, self.ff_own, self.size
        tokens, chips = self.tokens, len(self.plan.split)

        def kernel(s_ref, at_ref, sel_ref, *refs):
            token, weight = refs[:count], refs[count : 2 * count]
            extra = refs[2 * count : 2 * count + len(passed)]
            rows_ref, value_ref, *pass_refs, held_ref = refs[2 * count + len(passed) :]
            expert = pl.program_id(0)
            start, used = self.extent(s_ref, s_ref[0], expert)

            @pl.when(expert == 0)
            def _():
                for ref, out in zip((token[0], *extra), pass_refs):
                    out[...] = ref[...]
                value_ref[...] = jnp.zeros_like(value_ref)
                for b in range(self.ranks):
                    rows_of = slice(b * tokens, (b + 1) * tokens)
                    for o in range(count):
                        rows = jnp.dot(
                            sel_ref[b], token[o][rows_of, :], preferred_element_type=F32
                        ).astype(BF)
                        for e in range(each):
                            held_ref[e, b * CAP : (b + 1) * CAP, o * wide : (o + 1) * wide] = rows[
                                e * CAP : (e + 1) * CAP
                            ]

            rows = jnp.dot(
                self.packing(at_ref[0, expert]), held_ref[expert], preferred_element_type=F32
            ).astype(BF)
            rows_ref[0] = rows
            for i in range(2):
                value = sum(
                    jnp.dot(
                        rows[:, o * wide : (o + 1) * wide],
                        weight[o][0, i],
                        preferred_element_type=F32,
                    )
                    for o in range(count)
                ).astype(BF)
                for q in range(chips):
                    part = value[:, q * own : (q + 1) * own]
                    store_rows(value_ref.at[q], start, used, part, i * own)

        ins = [self.slots_in(), self.select_in()] + [self.whole(part) for part in parts]
        ins += [self.by_expert(piece) for piece in weights]
        ins += [self.whole(array) for array in passed]
        outs = [self.out_by_expert((each, size, count * wide), BF)]
        outs += [self.out_whole((chips, self.room, 2 * own), BF)]
        outs += [self.out_whole(array.shape, BF) for array in (parts[0], *passed)]
        flops = 2 * each * size * count * wide * (2 * self.ff + size)
        scratch = [pltpu.VMEM((each, size, count * wide), BF)]
        zero = jnp.int32(0)
        return self.call(
            kernel, "gate_up", place, zero, wait, each, ins, outs, scratch, flops
        )

    def inner(self, wait, place, chosen, value, base):
        each, own, room, tokens = self.each, self.ff_own, self.room, self.tokens
        steps = max(count for count in (1, 2, 3, 4) if room % (64 * count) == 0)
        size = room // steps
        tile = 64

        def kernel(s_ref, at_ref, sel_ref, chosen_ref, value_ref, base_ref, *refs):
            grads_ref, scaled_ref, table_ref, dots_ref = refs
            step = pl.program_id(0)
            for first in range(0, size, tile):
                rows = slice(first, first + tile)
                gate = value_ref[rows, :own].astype(F32)
                up = value_ref[rows, own:].astype(F32)
                base = base_ref[rows, :].astype(F32)
                chosen = chosen_ref[rows, :]
                sigma = 1.0 / (1.0 + jnp.exp(-gate))
                swish = gate * sigma
                active = swish * up
                grad = chosen * base
                grads_ref[rows, :own] = (
                    grad * up * sigma * (1.0 + gate * (1.0 - sigma))
                ).astype(BF)
                grads_ref[rows, own:] = (grad * swish).astype(BF)
                scaled_ref[rows, :] = (active * chosen).astype(BF)
                dots = jnp.sum(active * base, axis=1, keepdims=True)
                dots_ref[pl.ds(pl.multiple_of(step * size + first, tile), tile), :] = dots

            @pl.when(step == steps - 1)
            def _():
                for e in range(each):
                    start, used = self.extent(s_ref, s_ref[0], e)
                    dots = window(dots_ref, start, self.size).astype(BF)
                    dots = self.unpacked(at_ref[0, e], dots)
                    for b in range(self.ranks):
                        picks = sel_ref[b, e * CAP : (e + 1) * CAP, :].astype(F32)
                        table_ref[e, :, b * tokens : (b + 1) * tokens] = jnp.sum(
                            picks * dots[b * CAP : (b + 1) * CAP], axis=0, keepdims=True
                        )

        by_rows = lambda array: (array, (size, array.shape[1]), lambda c, s: (c, 0))
        ins = [self.slots_in(), self.select_in()]
        ins += [by_rows(array) for array in (chosen, value, base)]
        outs = [
            ((room, cols), BF, (size, cols), lambda c, s: (c, 0)) for cols in (2 * own, own)
        ]
        outs += [self.out_whole((each, 1, self.length), F32)]
        zero = jnp.int32(0)
        scratch = [pltpu.VMEM((room, 1), F32)]
        return self.call(kernel, "inner", place, zero, wait, steps, ins, outs, scratch=scratch)

    def rows_back(self, wait, place, grads, weights):
        each, count, wide, length = self.each, self.count, self.wide, self.length
        chips, tokens, own = len(self.plan.split), self.tokens, self.ff_own

        def kernel(s_ref, at_ref, sel_ref, grads_ref, *refs):
            weight = refs[:count]
            keep_ref, give_ref, held_ref = refs[count:]
            expert = pl.program_id(0)
            start, used = self.extent(s_ref, s_ref[0], expert)
            windows = [window(grads_ref.at[q], start, self.size) for q in range(chips)]
            windows = [
                jnp.concatenate([part[:, i * own : (i + 1) * own] for part in windows], axis=1)
                for i in range(2)
            ]
            rows = [
                sum(
                    lax.dot_general(
                        windows[i],
                        weight[o][0, i],
                        (((1,), (1,)), ((), ())),
                        preferred_element_type=F32,
                    )
                    for i in range(2)
                ).astype(BF)
                for o in range(count)
            ]
            rows = self.unpacked(at_ref[0, expert], jnp.concatenate(rows, axis=1)).astype(BF)
            for b in range(self.ranks):
                held_ref[b, pl.ds(pl.multiple_of(expert * CAP, CAP), CAP), :] = rows[
                    b * CAP : (b + 1) * CAP
                ]

            @pl.when(expert == each - 1)
            def _():
                for b in range(self.ranks):
                    out = jnp.dot(sel_ref[b], held_ref[b], preferred_element_type=F32).astype(BF)
                    keep_ref[b * tokens : (b + 1) * tokens, :] = out[:, :wide]
                    give_ref[b * tokens : (b + 1) * tokens, :] = out[:, wide:]

        ins = [self.slots_in(), self.select_t_in(), self.whole(grads)]
        ins += [self.by_expert(piece) for piece in weights]
        outs = [self.out_whole((length, wide), BF) for _ in range(2)]
        flops = 2 * each * self.size * count * wide * (2 * self.ff + self.size)
        scratch = [pltpu.VMEM((self.ranks, each * CAP, count * wide), BF)]
        zero = jnp.int32(0)
        return self.call(
            kernel, "rows_back", place, zero, wait, each, ins, outs, scratch, flops
        )

    def results(self, wait, place, me, scaled, downs):
        each, width, tokens, size = self.each, self.width, self.tokens, self.size
        half, count, own = self.ranks // 2, self.count, self.ff_own
        cols = min(512, width)

        def kernel(s_ref, at_ref, sel_ref, scaled_ref, *refs):
            down = refs[:count]
            keep_ref, give_ref, slots_ref, held_ref = refs[count:]

            @pl.when(pl.program_id(0) == 0)
            def _():
                for e in range(each):
                    start, used = self.extent(s_ref, s_ref[0], e)
                    value = window(scaled_ref, start, size)
                    slots_ref[e] = self.unpacked(at_ref[0, e], value).astype(BF)

            for e in range(each):
                weight = jnp.concatenate([ref[e, 0] for ref in down], axis=0)
                rows = jnp.dot(slots_ref[e], weight, preferred_element_type=F32).astype(BF)
                for b in range(self.ranks):
                    held_ref[b, e * CAP : (e + 1) * CAP, :] = rows[b * CAP : (b + 1) * CAP]
            for b in range(self.ranks):
                out = jnp.dot(sel_ref[b], held_ref[b], preferred_element_type=F32).astype(BF)
                other = s_ref[1] ^ b
                for side, ref in enumerate((keep_ref, give_ref)):

                    @pl.when(other % 2 == side)
                    def _():
                        ref[other // 2] = out

        ins = [self.slots_in(), self.select_t_in(), self.whole(scaled)]
        ins += [(piece, piece.shape[:3] + (cols,), lambda c, s: (0, 0, 0, c)) for piece in downs]
        out = ((half, tokens, width), BF, (half, tokens, cols), lambda c, s: (0, 0, c))
        outs = [out, out, self.out_whole((each, size, own), BF)]
        flops = 2 * each * size * width * (tokens + own)
        scratch = [pltpu.VMEM((self.ranks, each * CAP, cols), BF)]
        return self.call(
            kernel, "results", place, me, wait, width // cols, ins, outs, scratch, flops
        )

    def down_grads(self, wait, scaled, rows):
        each, count, width, planes = self.each, self.count, self.width, self.planes

        def kernel(s_ref, *refs):
            outs = refs[2 * planes :]
            left = jnp.concatenate([refs[d][0] for d in range(planes)], axis=0).T
            cols = min(512, width)
            for first in range(0, width, cols):
                part = slice(first, first + cols)
                right = jnp.concatenate([refs[planes + d][0, :, part] for d in range(planes)], axis=0)
                total = jnp.dot(left, right, preferred_element_type=F32).astype(BF)
                for o in range(count):
                    outs[o][0, 0, :, part] = total[o * self.ff_wide : (o + 1) * self.ff_wide]

        ins = [self.by_expert(array) for array in (*scaled, *rows)]
        outs = [self.out_by_expert((each, 1, self.ff_wide, width), BF) for _ in range(count)]
        flops = 2 * each * self.size * planes * width * self.ff_own
        zero = jnp.int32(0)
        return self.call(kernel, "down_grads", zero, zero, wait, each, ins, outs, flops=flops)

    def weight_grads(self, wait, places, rows, grads):
        each, count, wide, planes = self.each, self.count, self.wide, self.planes
        own, chips = self.ff_own, len(self.plan.split)
        tiles = 1 if planes * chips * self.room * own < 14 << 20 else chips
        at_once = chips // tiles

        def kernel(s_ref, *refs):
            outs = refs[2 * planes :]
            expert = lax.rem(pl.program_id(0), each)
            starts = [
                self.extent(s_ref, lax.rem(s_ref[0] + planes - d, planes), expert)[0]
                for d in range(planes)
            ]
            left = jnp.concatenate([refs[d][0] for d in range(planes)], axis=0).T
            for q in range(at_once):
                right = jnp.concatenate(
                    [
                        window(refs[planes + d].at[q], starts[d], self.size)
                        for d in range(planes)
                    ],
                    axis=0,
                )
                total = jnp.dot(left, right, preferred_element_type=F32).astype(BF)
                for o in range(count):
                    for i in range(2):
                        outs[o][0, i, :, q * own : (q + 1) * own] = total[
                            o * wide : (o + 1) * wide, i * own : (i + 1) * own
                        ]

        ins = [
            (array, (1,) + array.shape[1:], lambda e, s: (lax.rem(e, each), 0, 0)) for array in rows
        ]
        block = (at_once,) + grads[0].shape[1:]
        ins += [(array, block, lambda e, s: (lax.div(e, each), 0, 0), tiles == 1) for array in grads]
        out = (
            (each, 2, wide, self.ff),
            BF,
            (1, 2, wide, at_once * own),
            lambda e, s: (lax.rem(e, each), 0, 0, lax.div(e, each)),
        )
        outs = [out] * count
        flops = 4 * each * self.size * planes * count * wide * self.ff
        zero = jnp.int32(0)
        return self.call(
            kernel, "weight_grads", places[0], zero, wait, tiles * each, ins, outs, flops=flops
        )


def normed_blocks(near, far, masks, gain, me, wait):
    half, tokens, width = near.shape

    def kernel(s_ref, gain_ref, near_ref, far_ref, *refs):
        x_ref, hidden_ref = refs[len(wait) :]
        step = pl.program_id(0)
        for side, ref in enumerate((near_ref, far_ref)):

            @pl.when(step // half == side)
            def _():
                value = ref[0].astype(F32)
                scale = lax.rsqrt(jnp.mean(value * value, axis=-1, keepdims=True) + EPS)
                value = value * scale
                x_ref[...] = value.astype(BF)
                hidden_ref[...] = (value * gain_ref[...]).astype(BF)

    block = pl.BlockSpec((tokens, width), lambda n, s: (s[0] ^ s[1 + n], 0))
    shape = jax.ShapeDtypeStruct((2 * half * tokens, width), BF)
    order = list(masks) + [mask ^ 1 for mask in masks]
    return pl.pallas_call(
        kernel,
        grid_spec=pltpu.PrefetchScalarGridSpec(
            num_scalar_prefetch=1,
            grid=(2 * half,),
            in_specs=[
                pl.BlockSpec((1, width), lambda n, s: (0, 0)),
                pl.BlockSpec((1, tokens, width), lambda n, s: (jnp.minimum(n, half - 1), 0, 0)),
                pl.BlockSpec((1, tokens, width), lambda n, s: (jnp.maximum(n - half, 0), 0, 0)),
            ]
            + [pl.BlockSpec(memory_space=pl.ANY)] * len(wait),
            out_specs=[block, block],
        ),
        out_shape=[shape, shape],
        compiler_params=pltpu.CompilerParams(vmem_limit_bytes=32 << 20),
        cost_estimate=pl.CostEstimate(
            flops=0, bytes_accessed=12 * half * tokens * width, transcendentals=0
        ),
        name="normed_blocks",
    )(jnp.concatenate([me[None], jnp.array(order, jnp.int32)]), gain.reshape(1, width), near, far, *wait)


def local(
    layer_in,
    cotangent,
    file_lengths,
    routes,
    attn_gain,
    q_gain,
    k_gain,
    ffn_gain,
    w_q,
    w_k,
    w_v,
    w_o,
    router,
    expert_gate,
    expert_up,
    expert_down,
):
    planes = lax.axis_size("seq")
    ranks = lax.axis_size("ctx")
    plane = lax.axis_index("seq")
    me = lax.axis_index("ctx")
    nbits = ranks.bit_length() - 1
    tokens, width = layer_in.shape[1:]
    length = tokens * ranks
    total_tokens = length * planes
    blocks = planes * ranks
    wide = width // ranks
    heads = wide // HEAD_DIM
    experts = router.shape[1]
    per_plane = expert_gate.shape[0]
    ff = expert_gate.shape[2]
    ff_wide = ff // ranks
    scale = HEAD_DIM ** (-0.5)

    split_bits = list(range(1, nbits))

    w_own = jnp.stack([w_q, w_k, w_v, w_o])
    rows_own = w_own.shape[1]
    w_ctx = lax.all_to_all(
        jnp.transpose(w_own.reshape(4, rows_own, ranks, wide), (2, 0, 1, 3)),
        "ctx",
        split_axis=0,
        concat_axis=0,
        tiled=True,
    )

    small = [routes[0].T.astype(BF), router.T, jnp.stack([attn_gain, q_gain, k_gain, ffn_gain])]
    small_own = held(jnp.concatenate([part.reshape(-1) for part in small]), mark(w_ctx))
    small_all = lax.all_gather(small_own, "ctx")
    small_all = lax.all_gather(small_all, "seq").reshape(blocks, -1)
    ends = np.cumsum([part.size for part in small])
    routes_all = small_all[:, : ends[0]].reshape(blocks, -1, tokens).astype(jnp.int32)
    expert_ids = jnp.arange(experts, dtype=jnp.int32)
    counts_all = jnp.sum(
        (routes_all.reshape(blocks, 1, -1) == expert_ids[None, :, None]).astype(jnp.int32), axis=2
    )
    load = jnp.sum(counts_all, axis=0).reshape(planes, per_plane)
    earlier = jnp.arange(per_plane)[None, :] < jnp.arange(per_plane)[:, None]
    heavier = load[:, None, :] > load[:, :, None]
    heavier = heavier | ((load[:, None, :] == load[:, :, None]) & earlier)
    order = jnp.sum(heavier.astype(jnp.int32), axis=2)
    core_of = ((order + 1) // 2) % 2
    slot_of = core_of * (per_plane // 2) + order // 2
    numbers = jnp.arange(per_plane, dtype=jnp.int32)
    expert_at = jnp.sum(
        jnp.where(slot_of[:, None, :] == numbers[None, :, None], numbers[None, None, :], 0), axis=2
    )
    plan = Plan(split_bits[::-1], [0], pick(expert_at, plane, 0), me)
    plans = [plan]
    each, pieces = plan.each, plan.count
    ff_own = ff // len(plan.split)
    packed_gate_up = pack([expert_gate, expert_up], plans, ff_wide, ranks)
    packed_down = pack([expert_down], plans, 0, ranks)
    masks = list(range(0, ranks, 2))
    first_sent = mark(small_all)
    x_sent = held(layer_in[0], first_sent)
    x_parts = [x_sent if mask == 0 else swap(x_sent, mask) for mask in masks]
    x_near = jnp.stack(x_parts)
    cot_sent = held(cotangent[0], mark(x_parts[1]))
    cot_parts = [cot_sent if mask == 0 else swap(cot_sent, mask) for mask in masks]
    cot_near = jnp.stack(cot_parts)
    x_far = swap(x_near, 1)

    def gather_masks(value):
        near = jnp.stack([value if mask == 0 else swap(value, mask) for mask in masks])
        return near, swap(near, 1)

    def sum_masks(near, far):
        total = near.astype(F32) + swap(far, 1).astype(F32)
        return total[0] + sum(
            swap(total[number].astype(BF), masks[number]).astype(F32)
            for number in range(1, len(masks))
        )

    def by_rows(part):
        part = lax.all_gather(part, "seq", axis=0, tiled=False)
        return jnp.transpose(part, (2, 0, 1, 3, 4)).reshape(-1, width, wide)

    w_all = by_rows(w_ctx)
    w_qkv = w_all[:3]
    w_out = w_all[3].reshape(ranks, wide, wide)
    near_order = me ^ jnp.array(masks, jnp.int32)
    w_near, w_far = jnp.take(w_out, near_order, axis=0), jnp.take(w_out, near_order ^ 1, axis=0)
    router_all = small_all[:, ends[0] : ends[1]].reshape(blocks, experts, -1)
    router_all = jnp.transpose(router_all, (0, 2, 1)).reshape(width, experts)
    gains = small_all[:, ends[1] :].reshape(blocks, 4, -1)
    gains = jnp.transpose(gains, (1, 0, 2)).reshape(4, width).astype(F32)
    gain_attn = gains[0]
    own_gains = lax.dynamic_slice_in_dim(gains, me * wide, wide, 1)
    router_own = lax.dynamic_slice_in_dim(router_all, me * wide, wide, 0)
    gain_query, gain_key, gain_ffn = own_gains[1], own_gains[2], own_gains[3]
    x_normed, hidden = normed_blocks(
        x_near, x_far, masks, gain_attn, me, [packed_gate_up[0], packed_down[0]]
    )

    def own_columns(near, far):
        sides = [lax.dynamic_slice_in_dim(side, me * wide, wide, 2) for side in (near, far)]
        both = jnp.stack(sides, axis=1).reshape(ranks, tokens, wide)
        both = jnp.take(both, me ^ jnp.arange(ranks, dtype=jnp.int32), axis=0)
        return both.reshape(length, wide).astype(F32)

    sent_gate_up = send_pieces(packed_gate_up, plans)
    sent_down = send_pieces(packed_down, plans)

    places = [lax.rem(plane + planes - offset, planes) for offset in range(planes)]

    size = ranks * CAP
    lower = jnp.triu(jnp.ones((tokens, tokens), BF), 1)
    own_experts = plane * per_plane + plan.experts[:each]
    named = jnp.any(routes_all[:, None] == own_experts[None, :, None, None], axis=2)
    rank = mm("bet,tu->beu", named.astype(BF), lower)
    slot_numbers = jnp.arange(CAP, dtype=jnp.int32)
    select = named[:, :, None, :] & (rank[:, :, None, :] == slot_numbers[None, None, :, None])
    select = select.astype(BF).reshape(blocks, each * CAP, tokens)
    select_t = jnp.transpose(select, (0, 2, 1))
    in_block = jnp.sum(named.astype(jnp.int32), axis=2).reshape(planes, ranks, each)
    before = jnp.cumsum(in_block, axis=1) - in_block
    slot_at = jnp.where(
        slot_numbers < in_block[..., None], before[..., None] + slot_numbers, -1
    )
    slot_at = jnp.transpose(slot_at, (0, 2, 1, 3)).reshape(planes, each, 1, size)
    used = jnp.sum(in_block, axis=1)
    padded = (used + 15) // 16 * 16
    starts = jnp.cumsum(padded, axis=1) - padded
    layout = (
        jnp.concatenate([starts, used], axis=1).reshape(-1),
        slot_at,
        select,
        select_t,
    )

    by_chunk = jnp.sum(counts_all.reshape(planes, ranks, experts), axis=1)
    by_chunk = ((by_chunk + 15) // 16 * 16).reshape(planes, planes, per_plane)
    by_core = jnp.stack([jnp.sum(by_chunk * (core_of == core), axis=2) for core in range(2)])
    room_full = each * size + 64
    room_few = each * size * 11 // 16
    fits = jnp.max(by_core) <= room_few - 64

    cot_all = lax.all_gather(cot_near, "seq", axis=0)
    query_lin = mm("td,de->te", hidden, w_qkv[0])
    key_lin = mm("td,de->te", hidden, w_qkv[1])
    value_lin = mm("td,de->te", hidden, w_qkv[2])
    squares = jnp.stack([jnp.sum(query_lin * query_lin, -1), jnp.sum(key_lin * key_lin, -1)])
    squares = jnp.sum(lax.all_gather(squares, "ctx"), axis=0) / width
    query_scale, key_scale = lax.rsqrt(squares + EPS)[:, :, None]
    positions = jnp.arange(length, dtype=jnp.int32)
    cosine, sine = angles(positions)

    def by_head(value):
        return value.reshape(length, heads, HEAD_DIM)

    queries = rotate(by_head(query_lin * query_scale * gain_query), cosine, sine).astype(BF)
    keys = rotate(by_head(key_lin * key_scale * gain_key), cosine, sine).astype(BF)
    values = by_head(value_lin.astype(BF))
    lengths = file_lengths[0]
    files = segments(jnp.cumsum(lengths) - lengths, positions)
    allowed = (positions[None, :] <= positions[:, None]) & (files[None, :] == files[:, None])
    scores = mm("qhd,khd->hqk", queries, keys) * scale
    scores = jnp.where(allowed[None], scores, NEG)
    shifted = jnp.exp(scores - jnp.max(scores, axis=-1, keepdims=True))
    weights = (shifted / jnp.sum(shifted, axis=-1, keepdims=True)).astype(BF)
    attended = mm("hqk,khd->qhd", weights, values)
    mixed = attended.reshape(length, wide).astype(BF)
    mixed_near, mixed_far = gather_masks(mixed)
    own_inputs = own_columns(x_near, x_far)
    resid = own_inputs + mm("cld,cde->le", mixed_near, w_near) + mm("cld,cde->le", mixed_far, w_far)

    ffn_square = jnp.sum(resid * resid, -1)
    ffn_square = jnp.sum(lax.all_gather(ffn_square, "ctx"), axis=0) / width
    ffn_scale = lax.rsqrt(ffn_square + EPS)[:, None]
    normed = (resid * ffn_scale * gain_ffn).astype(BF)
    router_part = mm("td,de->et", normed, router_own)

    def find_probs():
        logits = router_part
        for bit in range(nbits):
            logits = logits + swap(logits, 1 << bit)
        shifted = jnp.exp(logits - jnp.max(logits, axis=0, keepdims=True))
        return shifted / jnp.sum(shifted, axis=0, keepdims=True)

    cot_far = swap(cot_near, 1)
    own_cot = own_columns(cot_near, cot_far)

    order_back = list(range(1, planes)) + [0]
    same_core = [list(range(core, ranks, 2)) for core in range(2)]

    def exchange_table(table):
        came = jnp.stack([to_earlier(table[d], d) for d in range(planes)])[None]
        for bit in range(nbits):
            came = jnp.concatenate([came, swap(came, 1 << bit)])
        came = jnp.take(came, me ^ jnp.arange(ranks, dtype=jnp.int32), axis=0)
        came = jnp.sum(came.reshape((ranks // 2, 2) + came.shape[1:]), axis=0)
        came = jnp.transpose(came, (1, 0, 2, 3)).reshape(planes, -1, length)
        turn = lax.rem(jnp.arange(planes, dtype=jnp.int32) + planes - plane, planes)
        came = jnp.take(came, turn, axis=0).reshape(experts, length)
        row_of = slot_of + per_plane * jnp.arange(planes, dtype=jnp.int32)[:, None]
        return jnp.take(came, row_of.reshape(-1), axis=0).T

    def run_experts(room):
        ops = Experts(plan, ranks, tokens, wide, ff, width, planes, room, layout)
        probs_t = find_probs()
        cot_all_far = swap(cot_all, 1)
        rows, cot_rows, terms, hidden_grads, scaled, at_slots = [], [], [], [], [], []
        table, back, lead_passed, probs_kept = [], {}, [normed], []
        sums = []

        def start_chunk(offset, wait):
            lead = lead_passed[-1] if offset == 0 else shift(lead_passed[-1])
            probs_kept.append(probs_t if offset == 0 else shift(probs_kept[-1]))
            found, value, *passed = ops.gate_up(
                [wait], places[offset], [lead, swap(lead, 1)], sent_gate_up
            )
            rows.append(found)
            lead_passed.append(passed[0])
            terms.append(
                lax.psum_scatter(
                    value, "ctx", scatter_dimension=0, axis_index_groups=same_core, tiled=False
                )
            )
            return found

        def middle_chunk(offset, wait, more=()):
            own_probs = jnp.take(probs_kept[offset], own_experts, axis=0)
            found, base, chosen = ops.cot_rows(
                [wait], places[offset], me, own_probs, cot_all, cot_all_far, masks, sent_down
            )
            cot_rows.append(found)
            grads, active, part = ops.inner([found, *more], places[offset], chosen, terms[offset], base)
            hidden_grads.append(
                lax.all_gather(grads, "ctx", axis=0, axis_index_groups=same_core)
            )
            scaled.append(active)
            table.append(part.reshape(each, length))
            return active

        def end_chunk(offset, wait, more=()):
            keep, give = ops.rows_back(
                [wait, *more], places[offset], hidden_grads[offset], sent_gate_up
            )
            back[offset] = keep.astype(F32) + swap(give, 1).astype(F32)
            return keep

        def finish_chunk(offset, wait):
            keep, give, found = ops.results(
                [wait], places[offset], me, scaled[offset], sent_down
            )
            at_slots.append(found)
            both = (keep.astype(F32) + swap(give, 1).astype(F32)).astype(BF)
            sums.append(both)
            return keep

        def pass_on(ring, offset):
            total = sums[offset].astype(F32) + (0.0 if ring is None else ring.astype(F32))
            return shift(total.astype(BF))

        ring = None
        wait = start_chunk(0, normed)
        for offset in range(1, planes):
            wait = start_chunk(offset, wait)
            wait = middle_chunk(offset - 1, wait)
            wait = finish_chunk(offset - 1, wait)
            if offset >= 2:
                wait = end_chunk(offset - 2, wait, [] if ring is None else [ring])
                ring = pass_on(ring, offset - 1)
        wait = middle_chunk(planes - 1, wait, [] if ring is None else [ring])
        wait = finish_chunk(planes - 1, wait)
        ring = pass_on(ring, planes - 1)
        wait = end_chunk(planes - 2, wait)
        down_parts = ops.down_grads([wait], at_slots, cot_rows)
        wait = end_chunk(planes - 1, down_parts[0], [ring])
        total = (ring.astype(F32) + sums[0].astype(F32)).astype(BF)
        gate_up_parts = ops.weight_grads([wait], places, rows, hidden_grads)
        carry = back[1]
        for offset in order_back[1:]:
            carry = shift(carry.astype(BF)).astype(F32) + back[offset]
        return carry, probs_t, total, exchange_table(table), down_parts, gate_up_parts

    grad_normed, probs_t, out_sum, grad_probs, down_parts, gate_up_parts = lax.cond(
        fits, lambda: run_experts(room_few), lambda: run_experts(room_full)
    )

    probs = probs_t.T
    grad_logits = (
        probs * (grad_probs - jnp.sum(probs * grad_probs, axis=-1, keepdims=True))
    ).astype(BF)
    grad_router = mm("td,te->de", normed, grad_logits)
    grad_normed = grad_normed + mm("te,de->td", grad_logits, router_own)

    down_parts = send_pieces(down_parts, plans)
    gate_up_parts = send_pieces(gate_up_parts, plans)

    def to_plane(part):
        size = part.shape[-2] // planes
        own = [lax.dynamic_slice_in_dim(part, p * size, size, part.ndim - 2) for p in places]
        carry = own[1]
        for offset in order_back[1:]:
            carry = shift(carry).astype(F32) + own[offset].astype(F32)
            carry = carry.astype(part.dtype)
        return carry

    def norm_back(values, own_scale, gain, grad, inner):
        return own_scale * gain * grad - values * (own_scale * own_scale * own_scale) * inner

    inner = jnp.sum(resid * gain_ffn * grad_normed, -1)
    inner = jnp.sum(lax.all_gather(inner, "ctx"), axis=0)
    grad_ffn_gain = jnp.sum(grad_normed * resid * ffn_scale, axis=0)
    grad_resid = own_cot + norm_back(resid, ffn_scale, gain_ffn, grad_normed, inner[:, None] / width)
    grad_attn = grad_resid.astype(BF)

    mixed_grads = [mm("le,cde->cld", grad_attn, side).astype(BF) for side in (w_near, w_far)]
    share_gate, share_up = unpack(gate_up_parts, plans, ff_wide, ranks, [mixed_grads[0]])
    grad_mixed = sum_masks(*mixed_grads) + mark(share_gate)
    grad_mixed = grad_mixed.astype(BF)
    grad_heads = by_head(grad_mixed)
    grad_weights = mm("qhd,khd->hqk", grad_heads, values)
    delta = jnp.sum(grad_heads.astype(F32) * attended, axis=-1).transpose(1, 0)[:, :, None]
    grad_scores = (weights.astype(F32) * (grad_weights - delta)).astype(BF)
    grad_query = mm("hqk,khd->qhd", grad_scores, keys) * scale
    grad_key = mm("hqk,qhd->khd", grad_scores, queries) * scale
    grad_value = mm("hqk,qhd->khd", weights, grad_heads).reshape(length, wide).astype(BF)
    grad_query = rotate(grad_query, cosine, -sine).reshape(length, wide)
    grad_key = rotate(grad_key, cosine, -sine).reshape(length, wide)
    inners = jnp.stack(
        [
            jnp.sum(query_lin * gain_query * grad_query, -1),
            jnp.sum(key_lin * gain_key * grad_key, -1),
        ]
    )
    inners = jnp.sum(lax.all_gather(inners, "ctx"), axis=0)[:, :, None] / width
    grad_query_gain = jnp.sum(grad_query * query_lin * query_scale, axis=0)
    grad_key_gain = jnp.sum(grad_key * key_lin * key_scale, axis=0)
    grad_query_b = norm_back(query_lin, query_scale, gain_query, grad_query, inners[0]).astype(BF)
    grad_key_b = norm_back(key_lin, key_scale, gain_key, grad_key, inners[1]).astype(BF)
    grads = (grad_query_b, grad_key_b, grad_value)
    share_down = unpack(down_parts, plans, 0, ranks, [grad_query_b])[0]
    both = held(jnp.stack([resid, grad_resid]), mark(inners)).reshape(2, ranks, tokens, wide).transpose(1, 0, 2, 3)
    both = lax.all_to_all(both, "ctx", split_axis=0, concat_axis=0, tiled=True)
    resid_own, grad_resid_own = jnp.transpose(both, (1, 2, 0, 3)).reshape(2, tokens, width)
    grad_hidden = sum(mm("te,de->td", grads[i], w_qkv[i]) for i in range(3))
    grad_attn_gain = jnp.sum(grad_hidden * x_normed.astype(F32), axis=0)
    grad_hidden = grad_hidden.astype(BF).reshape(ranks, tokens, width)
    grad_hidden = sum_masks(
        jnp.take(grad_hidden, near_order, axis=0), jnp.take(grad_hidden, near_order ^ 1, axis=0)
    )
    grad_out_w = [mm("cld,le->cde", side, grad_attn) for side in (mixed_near, mixed_far)]
    grad_out_w = jnp.stack(grad_out_w, axis=1).reshape(ranks, wide, wide)
    grad_out_w = jnp.take(grad_out_w, me ^ jnp.arange(ranks, dtype=jnp.int32), axis=0)
    grad_out_w = grad_out_w.reshape(width, wide)
    out_sum = out_sum.astype(F32) + mark(inners)
    out_blocks = [
        swap(out_sum[place_of].astype(BF), mask) for place_of, mask in enumerate(masks) if mask
    ]
    weight_grads = [mm("td,te->de", hidden, grad).astype(BF) for grad in grads]
    weight_grads = [
        to_plane(jnp.stack(weight_grads[:2])),
        to_plane(jnp.stack([weight_grads[2], grad_out_w.astype(BF)])),
    ]
    weight_grads = jnp.concatenate(weight_grads)
    weight_grads = weight_grads.reshape(4, ranks, rows_own, wide).transpose(1, 0, 2, 3)
    weight_grads = lax.all_to_all(weight_grads, "ctx", split_axis=0, concat_axis=0, tiled=True)
    weight_grads = weight_grads.transpose(1, 2, 0, 3).reshape(4, rows_own, width).astype(F32)

    own_x = layer_in[0].astype(F32)
    own_scale = lax.rsqrt(jnp.mean(own_x * own_x, axis=-1, keepdims=True) + EPS)
    inner = jnp.mean(own_x * gain_attn * grad_hidden, axis=-1, keepdims=True)
    grad_input = grad_resid_own + norm_back(own_x, own_scale, gain_attn, grad_hidden, inner)

    own_small = jnp.concatenate(
        [grad_router, jnp.stack([grad_query_gain, grad_key_gain, grad_ffn_gain], axis=1)], axis=1
    )
    small_grads = jnp.zeros((experts + 3, width), F32)
    small_grads = lax.dynamic_update_slice_in_dim(small_grads, own_small.T, me * wide, 1)
    small_grads = jnp.concatenate([small_grads, grad_attn_gain[None]], axis=0)
    small_grads = small_grads.reshape(experts + 4, planes, -1).transpose(1, 0, 2)
    parts_of = [pick(small_grads, p, 0) for p in places]
    carry = parts_of[1]
    for offset in order_back[1:]:
        carry = shift(carry) + parts_of[offset]
    carry = carry.reshape(experts + 4, ranks, -1).transpose(1, 0, 2)
    carry = lax.all_to_all(carry, "ctx", split_axis=0, concat_axis=0, tiled=True)
    small_grads = jnp.sum(carry, axis=0).T

    out_own = out_sum[0] + sum(block.astype(F32) for block in out_blocks)
    output = resid_own + out_own
    return (
        output.astype(BF)[None],
        grad_input.astype(BF)[None],
        small_grads[:, experts + 3],
        small_grads[:, experts],
        small_grads[:, experts + 1],
        small_grads[:, experts + 2],
        weight_grads[0],
        weight_grads[1],
        weight_grads[2],
        weight_grads[3],
        small_grads[:, :experts],
        share_gate,
        share_up,
        share_down,
        counts_all,
    )


def solution(mesh):
    tokens = P("seq", "ctx", None)
    flat = P(BOTH)
    rows = P(BOTH, None)
    return jax.shard_map(
        local,
        mesh=mesh,
        in_specs=(tokens, tokens, P("seq", None), tokens)
        + (flat,) * 4
        + (rows,) * 5
        + (tokens,) * 3,
        out_specs=(tokens, tokens) + (flat,) * 4 + (rows,) * 5 + (tokens,) * 3 + (P(),),
        check_vma=False,
    )
```
